512 devices in a mesh: grid: 32 (over x_lo, z), member: 16 (over x_hi, y, core).
Axes of the slice: x: 4 (x_hi: 2, x_lo: 2; x = x_hi * 2 + x_lo), y: 4, z: 16, core: 2. Of those that a mesh axis runs over, the one named last changes fastest.
Arguments:
- prior_sample_matrix: bfloat16 [512, 512, 1024], P('member', 'grid'), may hold values from -6 to 6
- cell_class: int32 [512, 1024], P('grid'), may hold values from 0 to 15
- diffusion_table: float32 [16], replicated, may hold values from 0.04 to 0.2
- velocity_table: float32 [2, 16], replicated, may hold values from -0.08 to 0.08
- obs_cells: int32 [32, 32, 128], P('grid'), may hold values from 0 to 16383
- obs_count: int32 [32, 32], P('grid'), may hold values from 16 to 128, as said below
- obs_value: float32 [32, 32, 128], P('grid'), may hold values from -6 to 6
- obs_scale: float32 [32, 32, 128], P('grid'), may hold values from 1 to 3
Outputs:
- predicted_samples: bfloat16 [512, 512, 1024], P('member', 'grid')
- posterior_mean_vector: float32 [512, 1024], P('grid')
- posterior_measured_mean: float32 [32, 32, 128], P('grid')
- mixing_factors: float32 [512], replicated
The draws below stay inside these ranges and needn't reach their ends.
Inputs may be any that keep to these rules, and one draw needn't show every extreme that they name: Slots at or beyond obs_count are unused; some owner has all 128 slots used from every source rank.
All inputs are finite; a program needn't handle non-finite values.
Results may differ from the reference program's by a relative error of at most 0.011.
Values may be sent and summed in bfloat16 or wider, within the bound.
A program may use at most 64 MiB of HBM per device.

```python
import math
import jax
import jax.numpy as jnp
from jax import lax

NC = 1024
ROWS_DEV = 16
STEPS = 6
CAP = 128
CLASSES = 16
NR = 512
MEMBERS = 512
N_GRID = 32


def draw_obs_count(key, part):
    key = jax.random.fold_in(key, 7)
    key_level, key_count, key_full = jax.random.split(key, 3)
    levels = jax.random.randint(key_level, (N_GRID, 1), 1, 5)
    raw_draw = jax.random.randint(key_count, (N_GRID, N_GRID), 0, 1048576)
    lower = levels * CAP // 8
    upper = levels * CAP // 4
    counts = lower + raw_draw % (upper - lower + 1)
    full_owner = jax.random.randint(key_full, (), 0, N_GRID)
    owner_index = jnp.arange(N_GRID, dtype=jnp.int32)[:, None]
    counts = jnp.where(owner_index == full_owner, CAP, counts)
    return counts.astype(jnp.int32)


def draw_obs_cells(key, part):
    key = jax.random.fold_in(key, 11)
    key_hot, key_pick, key_deep, key_deeper, key_mix, key_free = jax.random.split(key, 6)
    cell_total = ROWS_DEV * NC
    grid_shape = (N_GRID, N_GRID, CAP)
    hot_cells = jax.random.randint(key_hot, (N_GRID, 16), 0, cell_total)
    level_one = jax.random.randint(key_pick, grid_shape, 0, 16)
    level_two = jax.random.randint(key_deep, grid_shape, 0, 1048576) % (level_one + 1)
    level_three = jax.random.randint(key_deeper, grid_shape, 0, 1048576) % (level_two + 1)
    chosen_cells = jnp.take_along_axis(hot_cells, level_three.reshape(N_GRID, -1), axis=1).reshape(grid_shape)
    free_cells = jax.random.randint(key_free, grid_shape, 0, cell_total)
    mixture = jax.random.randint(key_mix, grid_shape, 0, 8)
    cell_pick = jnp.where(mixture < 7, chosen_cells, free_cells)
    flat_index = jnp.arange(N_GRID * N_GRID * CAP, dtype=jnp.int32).reshape(grid_shape)
    cell_pick = jnp.where(flat_index == 0, 0, cell_pick)
    cell_pick = jnp.where(flat_index == 1, cell_total - 1, cell_pick)
    return cell_pick.astype(jnp.int32)


def set_ends(drawn, stream_key, low, largest):
    longest = drawn.shape.index(max(drawn.shape))
    spots = []
    for shift in (0, 1):
        where = [jax.random.randint(jax.random.fold_in(stream_key, axis), (), 0, length) for axis, length in enumerate(drawn.shape)]
        where[longest] = (where[longest] + shift) % drawn.shape[longest]
        spots.append(tuple(where))
    return drawn.at[spots[0]].set(low).at[spots[1]].set(largest)


def block_scale(key, extent, pieces, least, top_value):
    def one(axis_at, parts):
        draws = jax.random.uniform(jax.random.fold_in(jax.random.fold_in(key, 6), axis_at), (parts,), jnp.float32, least / len(pieces), top_value / len(pieces))
        return jnp.repeat(jnp.exp(draws), extent[axis_at] // parts).reshape((-1,) + (1,) * (len(extent) - axis_at - 1))

    level = one(*pieces[0])
    for cut in pieces[1:]:
        level = level * one(*cut)
    return level


def gaussian(key, shape, width, most, cuts=(), held_as=jnp.bfloat16):
    array = width * jax.random.normal(key, shape, jnp.float32)
    if cuts:
        array = array * block_scale(key, shape, cuts, -0.22, 0.18)
    return jnp.clip(array, -most, most).astype(held_as)


def setup_inputs(seed: int = 0) -> dict:
    keys = jax.random.split(jax.random.key(seed), 9)
    prior_sample_matrix = gaussian(keys[0], (MEMBERS, NR, NC), 1.0, 6.0, ((0, 16), (1, 32)))
    cell_class = set_ends(jax.random.randint(keys[1], (NR, NC), 0, CLASSES), jax.random.fold_in(keys[1], 1), 0, CLASSES - 1).astype(jnp.int32)
    diffusion_table = jnp.clip(jnp.exp(jax.random.uniform(keys[2], (CLASSES,), jnp.float32, math.log(0.04), math.log(0.2))), 0.04, 0.2)
    velocity_table = jnp.clip(jax.random.uniform(keys[3], (2, CLASSES), jnp.float32, -0.08, 0.08), -0.08, 0.08)
    obs_cells = draw_obs_cells(jax.random.fold_in(keys[8], 71), 0)
    obs_count = draw_obs_count(jax.random.fold_in(keys[8], 71), 0)
    obs_value = gaussian(keys[6], (N_GRID, N_GRID, CAP), 1.0, 6.0, ((0, 32),), jnp.float32)
    obs_scale = jnp.clip(jnp.exp(math.log(3.0) - 1.0986123 * jax.random.uniform(keys[7], (N_GRID, N_GRID, CAP), jnp.float32) ** block_scale(keys[7], (N_GRID, N_GRID, CAP), ((0, 32),), -0.2, 0.2)), 1.0, 3.0)
    return dict(prior_sample_matrix=prior_sample_matrix, cell_class=cell_class, diffusion_table=diffusion_table, velocity_table=velocity_table, obs_cells=obs_cells, obs_count=obs_count, obs_value=obs_value, obs_scale=obs_scale)


HIGH = lax.Precision.HIGHEST

def advance(center, above_row, below_row, diffuse, drift_x, drift_y):
    lead = [(0, 0)] * (center.ndim - 1)
    left_col = jnp.pad(center, lead + [(1, 0)])[..., :-1]
    right_col = jnp.pad(center, lead + [(0, 1)])[..., 1:]
    result = (1.0 - 4.0 * diffuse) * center
    result = result + (diffuse + 0.5 * drift_y) * above_row + (diffuse - 0.5 * drift_y) * below_row
    return result + (diffuse + 0.5 * drift_x) * left_col + (diffuse - 0.5 * drift_x) * right_col

def solve_weights(gram_matrix, right_side):
    sample_count = gram_matrix.shape[0]
    system = gram_matrix + (sample_count - 1) * jnp.eye(sample_count, dtype=gram_matrix.dtype)
    factor = jnp.linalg.cholesky(system)
    column = right_side[:, None]
    inner = lax.linalg.triangular_solve(factor, column, left_side=True, lower=True)
    outer = lax.linalg.triangular_solve(factor, inner, left_side=True, lower=True, transpose_a=True)
    return outer[:, 0]

def reference(prior_sample_matrix, cell_class, diffusion_table, velocity_table, obs_cells, obs_count, obs_value, obs_scale):
    diffuse = diffusion_table[cell_class]
    drift_x = velocity_table[0][cell_class]
    drift_y = velocity_table[1][cell_class]

    def propagate_dynamics(member_state):
        ocean_vector = member_state.astype(jnp.float32)
        for repeat in range(STEPS):
            padded = jnp.pad(ocean_vector, ((1, 1), (0, 0)))
            ocean_vector = advance(ocean_vector, padded[:-2], padded[2:], diffuse, drift_x, drift_y)
        return ocean_vector.astype(jnp.bfloat16)
    predicted_samples = lax.map(propagate_dynamics, prior_sample_matrix)
    sample_count = predicted_samples.shape[0]
    offsets = jnp.arange(N_GRID, dtype=jnp.int32) * (ROWS_DEV * NC)
    source_first = obs_cells + offsets[:, None, None]
    cell_list = jnp.transpose(source_first, (1, 0, 2)).reshape(-1).astype(jnp.int32)
    raveled_vector = predicted_samples.reshape(sample_count, -1)
    sampled = jnp.take(raveled_vector, cell_list, axis=1).astype(jnp.float32)
    obs_mean = jnp.sum(sampled, axis=0) / sample_count
    slot_index = jnp.arange(CAP, dtype=jnp.int32)
    valid_slot = (slot_index[None, None, :] < obs_count[:, :, None]).astype(jnp.float32).reshape(-1)
    weight = obs_scale.reshape(-1) * valid_slot
    anomaly = sampled - obs_mean
    panel = lax.optimization_barrier((anomaly * weight).astype(jnp.bfloat16)).astype(jnp.float32)
    departure = (obs_value.reshape(-1) - obs_mean) * weight
    gram_matrix = jnp.dot(panel, panel.T, precision=HIGH)
    right_side = jnp.dot(panel, departure, precision=HIGH)
    mixing_factors = solve_weights(gram_matrix, right_side)
    sample_diffusivity = 1.0 / sample_count + mixing_factors - jnp.mean(mixing_factors)

    def running_summation(total, item):
        coef_one, field_one = item
        return (total + coef_one * field_one.astype(jnp.float32), None)
    posterior_mean_vector, discarded_output = lax.scan(running_summation, jnp.zeros(predicted_samples.shape[1:], jnp.float32), (sample_diffusivity, predicted_samples))
    posterior_measured_mean = (obs_mean + jnp.dot(mixing_factors, anomaly, precision=HIGH)).reshape(obs_value.shape)
    return (predicted_samples, posterior_mean_vector, posterior_measured_mean, mixing_factors)
```

```python
import functools

import jax
import jax.numpy as jnp
from jax import lax
from jax.experimental import pallas as pl
from jax.experimental.pallas import tpu as pltpu
from jax.sharding import PartitionSpec as P

STEPS = 6
MEMBERS = 512
HALO = 6
EXT = 28
NC = 1024
HIGH = lax.Precision.HIGHEST
MESH = pl.DeviceIdType.MESH
F32 = jnp.float32
BF16 = jnp.bfloat16
VMEM_LIMIT = 56 * 1024 * 1024


def place():
    g = lax.axis_index("grid")
    m = lax.axis_index("member")
    return g, m


def plane_of(g, m):
    return (g // 16) * 8 + (m // 8) * 4 + (m // 2) % 4


def plane_peer(p, g, m):
    return (p // 8) * 16 + g % 16, ((p // 4) % 2) * 8 + (p % 4) * 2 + m % 2


def z_reducer(j):
    return (8 * j) // 3


def remote(src, dst, send, recv, where):
    return pltpu.make_async_remote_copy(
        src_ref=src, dst_ref=dst, send_sem=send, recv_sem=recv, device_id=where, device_id_type=MESH
    )


def signal(sem, where):
    pl.semaphore_signal(sem, inc=1, device_id=where, device_id_type=MESH)


def split3(value):
    a = value.astype(BF16)
    rest = value - a.astype(F32)
    b = rest.astype(BF16)
    c = (rest - b.astype(F32)).astype(BF16)
    return a, b, c


def fill_coefs(g, cce, dif, vel, coef):
    for half in range(4):
        rows = pl.ds(half * 8, 8)
        cls = cce[rows, :]
        d = jnp.zeros((8, NC), F32)
        vx = jnp.zeros((8, NC), F32)
        vy = jnp.zeros((8, NC), F32)
        for c in range(16):
            hit = cls == c
            d = jnp.where(hit, dif[c], d)
            vx = jnp.where(hit, vel[0, c], vx)
            vy = jnp.where(hit, vel[1, c], vy)
        row = lax.broadcasted_iota(jnp.int32, (8, NC), 0) + (half * 8 - 8) + g * 16
        col = lax.broadcasted_iota(jnp.int32, (8, NC), 1)
        inside = jnp.logical_and(row >= 0, row < 512)
        coef[0, rows, :] = jnp.where(inside, 1.0 - 4.0 * d, 0.0)
        coef[1, rows, :] = jnp.where(inside, d + 0.5 * vy, 0.0)
        coef[2, rows, :] = jnp.where(inside, d - 0.5 * vy, 0.0)
        coef[3, rows, :] = jnp.where(jnp.logical_and(inside, col > 0), d + 0.5 * vx, 0.0)
        coef[4, rows, :] = jnp.where(jnp.logical_and(inside, col < NC - 1), d - 0.5 * vx, 0.0)


def stencil(src, r, q, c):
    sl = pl.ds(q * 8, 8)
    mid = src[r, sl, :]
    out = c[0] * mid
    out = out + c[1] * src[r - 1, sl, :] + c[2] * src[r + 1, sl, :]
    return out + c[3] * pltpu.roll(mid, 1, 1) + c[4] * pltpu.roll(mid, NC - 1, 1)


def main_kernel(
    stop, x_ref, cc_ref, dif, vel, cells, wv, pred, ff, samples,
    turn, a_buf, b_buf, coef, pbf, cce, hsend, hrecv, wrecv, sbuf, fpart, rcore, rplane, zsend, zrecv, fin,
    s_halo, r_halo, s_cls, r_cls, s_w, r_w, s_s, r_s, s_c, r_c, s_p, r_p, s_z, r_z, s_g, r_g, s_a, r_a, s_b, r_b,
):
    g, m = place()
    z, xl = g % 16, g // 16
    core = m % 2
    p = plane_of(g, m)
    other = m + 1 - 2 * core
    sender = g // 2 == m
    barrier = pltpu.get_barrier_semaphore()

    @pl.when(g > 0)
    def _():
        signal(barrier, (g - 1, m))

    @pl.when(g < 31)
    def _():
        signal(barrier, (g + 1, m))

    for o in range(2):
        @pl.when(2 * m + o != g)
        def _(o=o):
            signal(barrier, (2 * m + o, m))

    def greet(d, carry):
        signal(barrier, (g, (m + d) % 16))
        signal(barrier, plane_peer((p + d) % 16, g, m))
        signal(barrier, (xl * 16 + (z + d) % 16, m))
        return carry

    lax.fori_loop(1, 16, greet, 0)

    def unpack(i, carry):
        value = x_ref[i].astype(F32)
        for t in range(8):
            turn[t, pl.ds(i * 16, 16), :] = value[:, t * 128:(t + 1) * 128]
        return carry

    lax.fori_loop(0, 32, unpack, 0)

    def shuffle(r, carry):
        for q in range(4):
            for t in range(8):
                a_buf[r + HALO, pl.ds(q * 8, 8), t * 128:(t + 1) * 128] = turn[t, pl.ds(q * 128 + r, 8, stride=16), :]
        return carry

    lax.fori_loop(0, 16, shuffle, 0)
    for side in range(2):
        def pack(r, carry, side=side):
            hsend[side, r] = a_buf[r + HALO + side * 10].astype(BF16)
            return carry

        lax.fori_loop(0, HALO, pack, 0)

    count = 45 + (g > 0).astype(jnp.int32) + (g < 31).astype(jnp.int32) + 31 * sender.astype(jnp.int32)
    pl.semaphore_wait(barrier, count)

    up = remote(hsend.at[0], hrecv.at[1], s_halo.at[0], r_halo.at[1], (g - 1, m))
    down = remote(hsend.at[1], hrecv.at[0], s_halo.at[1], r_halo.at[0], (g + 1, m))
    cup = remote(cc_ref.at[pl.ds(0, 8)], cce.at[pl.ds(24, 8)], s_cls.at[0], r_cls.at[1], (g - 1, m))
    cdown = remote(cc_ref.at[pl.ds(8, 8)], cce.at[pl.ds(0, 8)], s_cls.at[1], r_cls.at[0], (g + 1, m))

    @pl.when(g > 0)
    def _():
        cup.start()
        up.start()

    @pl.when(g < 31)
    def _():
        cdown.start()
        down.start()

    @pl.when(sender)
    def _():
        def give(d, carry):
            s = (g + d) % 32
            remote(wv.at[s], wrecv.at[g % 2], s_w.at[d], r_w.at[g % 2], (s, m)).start()
            return carry

        lax.fori_loop(1, 32, give, 0)
        wrecv[g % 2] = wv[g]

    cce[pl.ds(8, 16), :] = cc_ref[...]

    @pl.when(g == 0)
    def _():
        hrecv[0] = jnp.zeros((HALO, 32, NC), BF16)
        cce[pl.ds(0, 8), :] = jnp.zeros((8, NC), jnp.int32)

    @pl.when(g == 31)
    def _():
        hrecv[1] = jnp.zeros((HALO, 32, NC), BF16)
        cce[pl.ds(24, 8), :] = jnp.zeros((8, NC), jnp.int32)

    @pl.when(g > 0)
    def _():
        cup.wait_send()
        cdown.wait_recv()
        up.wait_send()
        down.wait_recv()

    @pl.when(g < 31)
    def _():
        cdown.wait_send()
        cup.wait_recv()
        down.wait_send()
        up.wait_recv()

    fill_coefs(g, cce, dif, vel, coef)
    for side in range(2):
        def widen(r, carry, side=side):
            a_buf[r + side * 22] = hrecv[side, r].astype(F32)
            return carry

        lax.fori_loop(0, HALO, widen, 0)

    bufs = (a_buf, b_buf)
    for k in range(STEPS):
        src, dst = bufs[k % 2], bufs[(k + 1) % 2]

        def line(r, carry, src=src, dst=dst, k=k):
            c = [jnp.broadcast_to(coef[i, pl.ds(r + 2, 1), :], (8, NC)) for i in range(5)]
            rows = []
            for q in range(4):
                out = stencil(src, r, q, c)
                if k < STEPS - 1:
                    dst[r, pl.ds(q * 8, 8), :] = out
                else:
                    for t in range(8):
                        turn[t, pl.ds(q * 128 + r - HALO, 8, stride=16), :] = out[:, t * 128:(t + 1) * 128]
                    rows.append(out)
            if k == STEPS - 1:
                pbf[pl.ds((r - HALO) * 32, 32), :] = jnp.concatenate(rows, axis=0).astype(BF16)
            return carry

        lax.fori_loop(k + 1, EXT - 1 - k, line, 0)

    def finish(i, carry):
        for t in range(8):
            pred[i, :, t * 128:(t + 1) * 128] = turn[t, pl.ds(i * 16, 16), :].astype(BF16)
        return carry

    lax.fori_loop(0, 32, finish, 0)

    def sample(chunk):
        cell = cells[chunk]
        col = cell & (NC - 1)
        row = cell >> 10
        onehot = (lax.broadcasted_iota(jnp.int32, (NC, 256), 0) == col).astype(F32).astype(BF16)
        wide = jnp.dot(pbf[...], onehot, preferred_element_type=F32)
        total = jnp.zeros((32, 256), F32)
        for r in range(16):
            total = total + jnp.where(row == r, wide[r * 32:(r + 1) * 32], 0.0)
        return total.astype(BF16)

    def scatter(d, carry):
        peer = (m + d) % 16
        sbuf[d] = sample(peer)
        remote(sbuf.at[d], samples.at[m], s_s.at[d], r_s.at[m], (g, peer)).start()
        return carry

    lax.fori_loop(1, 16, scatter, 0)
    samples[m] = sample(m)

    @pl.when(sender)
    def _():
        def given(d, carry):
            remote(wv.at[g], wrecv.at[g % 2], s_w.at[d], r_w.at[g % 2], (g, m)).wait_send()
            return carry

        lax.fori_loop(1, 32, given, 0)

    for o in range(2):
        @pl.when(2 * m + o != g)
        def _(o=o):
            remote(wv.at[g], wrecv.at[o], s_w.at[0], r_w.at[o], (g, m)).wait_recv()

    def scattered(d, carry):
        peer = (m + d) % 16
        c = remote(sbuf.at[d], samples.at[peer], s_s.at[d], r_s.at[peer], (g, peer))
        c.wait_send()
        c.wait_recv()
        return carry

    lax.fori_loop(1, 16, scattered, 0)

    sampled = samples[...].reshape(MEMBERS, 256).astype(F32)
    mean = jnp.sum(sampled, axis=0, keepdims=True) / MEMBERS
    weight = jnp.concatenate([wrecv[0, :, 0:128], wrecv[1, :, 0:128]], axis=1)
    value = jnp.concatenate([wrecv[0, :, 128:256], wrecv[1, :, 128:256]], axis=1)
    panel = ((sampled - mean) * weight).astype(BF16)
    dep = (value - mean) * weight
    parts = split3(dep)
    line_at = lax.broadcasted_iota(jnp.int32, (128, 256), 0)
    dep_one = jnp.zeros((128, 256), F32)
    dep_two = jnp.zeros((128, 256), F32)
    for i in range(3):
        dep_one = jnp.where(line_at == i, parts[i].astype(F32), dep_one)
        dep_two = jnp.where(line_at == 64 + i, parts[i].astype(F32), dep_two)
    dep_one = dep_one.astype(BF16)
    dep_two = dep_two.astype(BF16)
    blk = [panel[i * 128:(i + 1) * 128] for i in range(4)]

    def outer(a, b):
        return lax.dot_general(a, b, (((1,), (1,)), ((), ())), preferred_element_type=F32)

    pairs = (
        ((0, 0), (0, 1), (0, 2), (0, 3), (3, 3)),
        ((1, 1), (1, 2), (1, 3), (2, 2), (2, 3)),
    )
    for h in range(2):
        for t in range(5):
            i, j = pairs[h][t]
            fpart[h, :, t] = outer(blk[i], blk[j]).reshape(16, 8, 128)
        fpart[h, :, 5] = (outer(blk[h], dep_one) + outer(blk[3 - h], dep_two)).reshape(16, 8, 128)

    swap = remote(fpart.at[1 - core], rcore, s_c.at[0], r_c.at[0], (g, other))
    swap.start()
    swap.wait()

    def pair_sum(i, carry):
        rcore[i] = rcore[i] + fpart[core, i]
        return carry

    lax.fori_loop(0, 16, pair_sum, 0)

    def plane_give(d, carry):
        q = (p + d) % 16
        remote(rcore.at[q], rplane.at[p], s_p.at[d], r_p.at[p], plane_peer(q, g, m)).start()
        return carry

    lax.fori_loop(1, 16, plane_give, 0)

    def plane_take(d, total):
        q = (p + d) % 16
        c = remote(rcore.at[q], rplane.at[q], s_p.at[d], r_p.at[q], plane_peer(q, g, m))
        c.wait_recv()
        return total + rplane[q]

    zsend[...] = lax.fori_loop(1, 16, plane_take, rcore[p])

    for j in range(6):
        @pl.when(z != z_reducer(j))
        def _(j=j):
            remote(zsend.at[j], zrecv.at[z], s_z.at[j], r_z.at[z], (xl * 16 + z_reducer(j), m)).start()

    for j in range(6):
        @pl.when(z == z_reducer(j))
        def _(j=j):
            def z_take(d, total):
                q = (z + d) % 16
                remote(zsend.at[j], zrecv.at[q], s_z.at[j], r_z.at[q], (xl * 16 + q, m)).wait_recv()
                return total + zrecv[q]

            fin[p, j] = lax.fori_loop(1, 16, z_take, zsend[j])

            def z_give(d, carry):
                q = (z + d) % 16
                remote(fin.at[p, j], fin.at[p, j], s_g.at[d], r_g.at[j], (xl * 16 + q, m)).start()
                return carry

            lax.fori_loop(1, 16, z_give, 0)

    for j in range(6):
        @pl.when(z != z_reducer(j))
        def _(j=j):
            remote(fin.at[p, j], fin.at[p, j], s_g.at[0], r_g.at[j], (xl * 16 + z_reducer(j), m)).wait_recv()

    def plane_send(d, carry):
        q = (p + d) % 16
        remote(fin.at[p], fin.at[p], s_a.at[d], r_a.at[p], plane_peer(q, g, m)).start()
        return carry

    lax.fori_loop(1, 16, plane_send, 0)

    def plane_got(d, carry):
        q = (p + d) % 16
        remote(fin.at[q], fin.at[q], s_a.at[d], r_a.at[q], plane_peer(q, g, m)).wait_recv()
        return carry

    lax.fori_loop(1, 16, plane_got, 0)
    back = remote(fin, ff.at[core], s_b.at[0], r_b.at[0], (g, other))
    back.start()

    def keep(i, carry):
        ff[core, i] = fin[i]
        return carry

    lax.fori_loop(0, 16, keep, 0)
    back.wait()

    def drain(d, carry):
        q = (p + d) % 16
        remote(rcore.at[q], rplane.at[q], s_p.at[d], r_p.at[q], plane_peer(q, g, m)).wait_send()
        remote(fin.at[p], fin.at[p], s_a.at[d], r_a.at[p], plane_peer(q, g, m)).wait_send()
        return carry

    lax.fori_loop(1, 16, drain, 0)
    for j in range(6):
        @pl.when(z != z_reducer(j))
        def _(j=j):
            remote(zsend.at[j], zrecv.at[z], s_z.at[j], r_z.at[z], (xl * 16 + z_reducer(j), m)).wait_send()

        @pl.when(z == z_reducer(j))
        def _(j=j):
            def z_given(d, carry):
                q = (z + d) % 16
                remote(fin.at[p, j], fin.at[p, j], s_g.at[d], r_g.at[j], (xl * 16 + q, m)).wait_send()
                return carry

            lax.fori_loop(1, 16, z_given, 0)


def run_main(x, cc, dif, vel, cells, wv, stop=None):
    vmem = pl.BlockSpec(memory_space=pltpu.VMEM)
    smem = pl.BlockSpec(memory_space=pltpu.SMEM)
    dma = pltpu.SemaphoreType.DMA
    return pl.pallas_call(
        functools.partial(main_kernel, stop),
        out_shape=(
            jax.ShapeDtypeStruct((32, 16, NC), BF16),
            jax.ShapeDtypeStruct((2, 16, 6, 8, 128), F32),
            jax.ShapeDtypeStruct((16, 32, 256), BF16),
        ),
        in_specs=[vmem, vmem, smem, smem, vmem, vmem],
        out_specs=(vmem, vmem, vmem),
        scratch_shapes=[
            pltpu.VMEM((8, 512, 128), F32),
            pltpu.VMEM((EXT, 32, NC), F32),
            pltpu.VMEM((EXT, 32, NC), F32),
            pltpu.VMEM((5, 32, NC), F32),
            pltpu.VMEM((512, NC), BF16),
            pltpu.VMEM((32, NC), jnp.int32),
            pltpu.VMEM((2, HALO, 32, NC), BF16),
            pltpu.VMEM((2, HALO, 32, NC), BF16),
            pltpu.VMEM((2, 1, 256), F32),
            pltpu.VMEM((16, 32, 256), BF16),
            pltpu.VMEM((2, 16, 6, 8, 128), F32),
            pltpu.VMEM((16, 6, 8, 128), F32),
            pltpu.VMEM((16, 6, 8, 128), F32),
            pltpu.VMEM((6, 8, 128), F32),
            pltpu.VMEM((16, 8, 128), F32),
            pltpu.VMEM((16, 6, 8, 128), F32),
            dma((2,)), dma((2,)), dma((2,)), dma((2,)), dma((32,)), dma((2,)), dma((16,)), dma((16,)),
            dma((1,)), dma((1,)), dma((16,)), dma((16,)), dma((6,)), dma((16,)), dma((16,)), dma((6,)),
            dma((16,)), dma((16,)), dma((1,)), dma((1,)),
        ],
        compiler_params=pltpu.CompilerParams(
            collective_id=0, has_side_effects=True, vmem_limit_bytes=VMEM_LIMIT
        ),
    )(x, cc, dif, vel, cells, wv)


def inverse(a):
    row = lax.broadcasted_iota(jnp.int32, (128, 128), 0)
    col = lax.broadcasted_iota(jnp.int32, (128, 128), 1)
    diag = jnp.where(row == col, a, 0.0)
    s_col = lax.rsqrt(jnp.sum(diag, axis=1, keepdims=True))
    s_row = lax.rsqrt(jnp.sum(diag, axis=0, keepdims=True))
    lane = lax.broadcasted_iota(jnp.int32, (1, 128), 1)
    line = lax.broadcasted_iota(jnp.int32, (128, 1), 0)

    def sweep(_, a):
        for k in range(8):
            r = a[k:k + 1, :]
            c = a[:, k:k + 1]
            d = a[k:k + 1, k:k + 1]
            inv = 1.0 / d
            r = jnp.where(lane == k, 1.0 + inv, r * inv)
            c = jnp.where(line == k, d - 1.0, c)
            a = a - c * r
        a = jnp.concatenate([a[8:], a[:8]], axis=0)
        return pltpu.roll(a, 120, 1)

    a = lax.fori_loop(0, 16, sweep, a * s_col * s_row)
    return a * s_col * s_row


def mm(a, b):
    return jnp.dot(a, b, precision=HIGH, preferred_element_type=F32)


def solve_kernel(ff, xcol, xrow):
    row = lax.broadcasted_iota(jnp.int32, (128, 128), 0)
    col = lax.broadcasted_iota(jnp.int32, (128, 128), 1)
    ridge = jnp.where(row == col, float(MEMBERS - 1), 0.0)

    def tile(h, t):
        return ff[h, :, t].reshape(128, 128)

    def right(h, first):
        part = tile(h, 5)
        keep = jnp.logical_and(col >= first, col < first + 3)
        return jnp.broadcast_to(jnp.sum(jnp.where(keep, part, 0.0), axis=1, keepdims=True), (128, 128))

    a = {
        (0, 0): tile(0, 0), (0, 1): tile(0, 1), (0, 2): tile(0, 2), (0, 3): tile(0, 3), (3, 3): tile(0, 4),
        (1, 1): tile(1, 0), (1, 2): tile(1, 1), (1, 3): tile(1, 2), (2, 2): tile(1, 3), (2, 3): tile(1, 4),
    }
    b = [right(0, 0), right(1, 0), right(1, 64), right(0, 64)]
    w = {}
    y = []
    for k in range(4):
        d = inverse(a[k, k] + ridge)
        y.append(mm(d, b[k]))
        for j in range(k + 1, 4):
            w[k, j] = mm(d, a[k, j])
        for i in range(k + 1, 4):
            t = a[k, i].T
            b[i] = b[i] - mm(t, y[k])
            for j in range(i, 4):
                a[i, j] = a[i, j] - mm(t, w[k, j])
    x = [None] * 4
    for k in reversed(range(4)):
        total = y[k]
        for j in range(k + 1, 4):
            total = total - mm(w[k, j], x[j])
        x[k] = total
    for k in range(4):
        xcol[pl.ds(k * 128, 128), :] = x[k]
        xrow[:, k * 128:(k + 1) * 128] = x[k].T[0:8, :]


def run_solve(ff):
    vmem = pl.BlockSpec(memory_space=pltpu.VMEM)
    return pl.pallas_call(
        solve_kernel,
        out_shape=(jax.ShapeDtypeStruct((512, 128), F32), jax.ShapeDtypeStruct((8, 512), F32)),
        in_specs=[vmem],
        out_specs=(vmem, vmem),
        compiler_params=pltpu.CompilerParams(vmem_limit_bytes=VMEM_LIMIT),
    )(ff)


def final_kernel(
    xcol, xrow, pred, samples, mean_out, obs_out,
    part, rpart, gath, osend, orecv, s_r, r_r, s_g, r_g, s_o, r_o,
):
    g, m = place()
    barrier = pltpu.get_barrier_semaphore()

    def greet(d, carry):
        signal(barrier, (g, (m + d) % 16))
        return carry

    lax.fori_loop(1, 16, greet, 0)

    def greet_far(s, carry):
        @pl.when(jnp.logical_or(s != g, m != g // 2))
        def _():
            signal(barrier, (s, g // 2))
        return carry

    lax.fori_loop(0, 32, greet_far, 0)

    x_all = xcol[...]
    shift = 1.0 / MEMBERS - jnp.sum(x_all[:, 0:1], axis=0, keepdims=True) / MEMBERS
    mine = xcol[pl.ds(m * 32, 32), :][:, 0:1] + shift

    total = jnp.zeros((16, NC), F32)
    for i in range(32):
        total = total + mine[i:i + 1, 0:1] * pred[i].astype(F32)
    for r in range(16):
        part[r] = total[r:r + 1, :]
    coef_row = xrow[...] + shift
    slot = jnp.zeros((8, 256), F32)
    flat = samples[...].reshape(MEMBERS, 256)
    for piece in split3(coef_row):
        slot = slot + jnp.dot(piece, flat, preferred_element_type=F32)
    osend[0] = slot[0:1, 0:128]
    osend[1] = slot[0:1, 128:256]

    selfish = (g // 2 == m).astype(jnp.int32)
    pl.semaphore_wait(barrier, 47 - selfish)

    def give(d, carry):
        q = (m + d) % 16
        remote(part.at[q], rpart.at[m], s_r.at[d], r_r.at[m], (g, q)).start()
        return carry

    lax.fori_loop(1, 16, give, 0)

    def show(d, carry):
        o = 2 * m + d // 16
        q = d % 16

        @pl.when(jnp.logical_or(o != g, q != m))
        def _():
            remote(osend.at[d // 16], orecv.at[g], s_o.at[d], r_o.at[g], (o, q)).start()

        @pl.when(jnp.logical_and(o == g, q == m))
        def _():
            orecv[g] = osend[d // 16]
        return carry

    lax.fori_loop(0, 32, show, 0)

    def take(d, total):
        q = (m + d) % 16
        remote(part.at[q], rpart.at[q], s_r.at[d], r_r.at[q], (g, q)).wait_recv()
        return total + rpart[q]

    gath[m] = lax.fori_loop(1, 16, take, part[m])

    def spread(d, carry):
        q = (m + d) % 16
        remote(gath.at[m], gath.at[m], s_g.at[d], r_g.at[m], (g, q)).start()
        return carry

    lax.fori_loop(1, 16, spread, 0)

    def got(d, carry):
        q = (m + d) % 16
        remote(gath.at[q], gath.at[q], s_g.at[d], r_g.at[q], (g, q)).wait_recv()
        return carry

    lax.fori_loop(1, 16, got, 0)

    def seen(s, carry):
        @pl.when(jnp.logical_or(s != g, m != g // 2))
        def _():
            remote(osend.at[0], orecv.at[s], s_o.at[0], r_o.at[s], (s, g // 2)).wait_recv()
        return carry

    lax.fori_loop(0, 32, seen, 0)
    for r in range(16):
        mean_out[r:r + 1, :] = gath[r]
    for s in range(32):
        obs_out[s:s + 1, :] = orecv[s]

    def drain(d, carry):
        q = (m + d) % 16
        remote(part.at[q], rpart.at[q], s_r.at[d], r_r.at[q], (g, q)).wait_send()
        remote(gath.at[m], gath.at[m], s_g.at[d], r_g.at[m], (g, q)).wait_send()
        return carry

    lax.fori_loop(1, 16, drain, 0)

    def shown(d, carry):
        o = 2 * m + d // 16
        q = d % 16

        @pl.when(jnp.logical_or(o != g, q != m))
        def _():
            remote(osend.at[d // 16], orecv.at[g], s_o.at[d], r_o.at[g], (o, q)).wait_send()
        return carry

    lax.fori_loop(0, 32, shown, 0)


def run_final(xcol, xrow, pred, samples):
    vmem = pl.BlockSpec(memory_space=pltpu.VMEM)
    dma = pltpu.SemaphoreType.DMA
    return pl.pallas_call(
        final_kernel,
        out_shape=(jax.ShapeDtypeStruct((16, NC), F32), jax.ShapeDtypeStruct((32, 128), F32)),
        in_specs=[vmem] * 4,
        out_specs=(vmem, vmem),
        scratch_shapes=[
            pltpu.VMEM((16, 1, NC), F32),
            pltpu.VMEM((16, 1, NC), F32),
            pltpu.VMEM((16, 1, NC), F32),
            pltpu.VMEM((2, 1, 128), F32),
            pltpu.VMEM((32, 1, 128), F32),
            dma((16,)), dma((16,)), dma((16,)), dma((16,)), dma((32,)), dma((32,)),
        ],
        compiler_params=pltpu.CompilerParams(
            collective_id=1, has_side_effects=True, vmem_limit_bytes=VMEM_LIMIT
        ),
    )(xcol, xrow, pred, samples)


def local(
    prior_sample_matrix, cell_class, diffusion_table, velocity_table, obs_cells, obs_count, obs_value, obs_scale
):
    slot_index = jnp.arange(128, dtype=jnp.int32)
    valid = (slot_index[None, :] < obs_count[0][:, None]).astype(F32)
    wv = jnp.concatenate([obs_scale[0] * valid, obs_value[0]], axis=1).reshape(32, 1, 256)
    cells = obs_cells.reshape(16, 1, 256)
    pred, ff, samples = run_main(prior_sample_matrix, cell_class, diffusion_table, velocity_table, cells, wv)
    xcol, xrow = run_solve(ff)
    mean, obs = run_final(xcol, xrow, pred, samples)
    return pred, mean, obs.reshape(1, 32, 128), xrow[0]


def solution(mesh):
    in_specs = (
        P("member", "grid", None),
        P("grid", None),
        P(),
        P(),
        P("grid", None, None),
        P("grid", None),
        P("grid", None, None),
        P("grid", None, None),
    )
    out_specs = (P("member", "grid", None), P("grid", None), P("grid", None, None), P())
    return jax.shard_map(local, mesh=mesh, in_specs=in_specs, out_specs=out_specs, check_vma=False)
```

```python
import functools

import jax
import jax.numpy as jnp
from jax import lax
from jax.experimental import pallas as pl
from jax.experimental.pallas import tpu as pltpu
from jax.sharding import PartitionSpec as P

STEPS = 6
MEMBERS = 512
HALO = 6
EXT = 28
NC = 1024
HIGH = lax.Precision.HIGHEST
MESH = pl.DeviceIdType.MESH
F32 = jnp.float32
BF16 = jnp.bfloat16
VMEM_LIMIT = 56 * 1024 * 1024


def place():
    g = lax.axis_index("grid")
    m = lax.axis_index("member")
    return g, m


def plane_of(g, m):
    return (g // 16) * 8 + (m // 8) * 4 + (m // 2) % 4


def plane_peer(p, g, m):
    return (p // 8) * 16 + g % 16, ((p // 4) % 2) * 8 + (p % 4) * 2 + m % 2


def z_reducer(j):
    return (8 * j) // 3


def remote(src, dst, send, recv, where):
    return pltpu.make_async_remote_copy(
        src_ref=src, dst_ref=dst, send_sem=send, recv_sem=recv, device_id=where, device_id_type=MESH
    )


def signal(sem, where):
    pl.semaphore_signal(sem, inc=1, device_id=where, device_id_type=MESH)


def split3(value):
    a = value.astype(BF16)
    rest = value - a.astype(F32)
    b = rest.astype(BF16)
    c = (rest - b.astype(F32)).astype(BF16)
    return a, b, c


def across(value):
    return (value % 8) * 128 + value // 8


def fill_coefs(g, cce, dif, vel, coef):
    place_of = lax.broadcasted_iota(jnp.int32, (8, NC), 1)
    for quarter in range(4):
        rows = pl.ds(quarter * 8, 8)
        cls = cce[rows, :]
        d = jnp.zeros((8, NC), F32)
        vx = jnp.zeros((8, NC), F32)
        vy = jnp.zeros((8, NC), F32)
        for c in range(16):
            hit = cls == float(c)
            d = jnp.where(hit, dif[c], d)
            vx = jnp.where(hit, vel[0, c], vx)
            vy = jnp.where(hit, vel[1, c], vy)
        row = lax.broadcasted_iota(jnp.int32, (8, NC), 0) + (quarter * 8 - 8) + g * 16
        inside = jnp.logical_and(row >= 0, row < 512)
        values = (
            jnp.where(inside, 1.0 - 4.0 * d, 0.0),
            jnp.where(inside, d + 0.5 * vy, 0.0),
            jnp.where(inside, d - 0.5 * vy, 0.0),
            jnp.where(jnp.logical_and(inside, place_of > 0), d + 0.5 * vx, 0.0),
            jnp.where(jnp.logical_and(inside, place_of < NC - 1), d - 0.5 * vx, 0.0),
        )
        for i in range(5):
            for t in range(8):
                coef[t, quarter * 8:quarter * 8 + 8, i, :] = values[i][:, t * 128:(t + 1) * 128]


def inverse(a):
    lane = lax.broadcasted_iota(jnp.int32, (8, 128), 1)
    line = lax.broadcasted_iota(jnp.int32, (8, 128), 0)
    v = [a[8 * i:8 * i + 8] for i in range(16)]
    for t in range(16):
        col = [
            [jnp.broadcast_to(v[i][:, 8 * t + j:8 * t + j + 1], (8, 128)) for i in range(16)] for j in range(8)
        ]
        inside = jnp.logical_and(lane >= 8 * t, lane < 8 * t + 8)
        u = jnp.where(inside, (lane - 8 * t == line).astype(F32), v[t])
        k = [col[j][t] for j in range(8)]
        for s in range(8):
            inv = 1.0 / k[s][s:s + 1]
            here = line == s
            for j in range(s + 1, 8):
                r = k[j][s:s + 1] * inv
                k[j] = jnp.where(here, r, k[j] - k[s] * r)
            r = u[s:s + 1] * inv
            u = jnp.where(here, r, u - k[s] * r)
        rows = [jnp.broadcast_to(u[s:s + 1], (8, 128)) for s in range(8)]
        for d in range(1, 16):
            i = (t + d) % 16
            w = jnp.where(inside, 0.0, v[i])
            x0 = col[0][i] * rows[0] + col[1][i] * rows[1]
            x1 = col[2][i] * rows[2] + col[3][i] * rows[3]
            x2 = col[4][i] * rows[4] + col[5][i] * rows[5]
            x3 = col[6][i] * rows[6] + col[7][i] * rows[7]
            v[i] = w - ((x0 + x1) + (x2 + x3))
        v[t] = u
    return jnp.concatenate(v, axis=0)


def mm(a, b):
    return jnp.dot(a, b, precision=HIGH, preferred_element_type=F32)


def solve(ff, asc, wsc, xcol):
    row = lax.broadcasted_iota(jnp.int32, (128, 128), 0)
    col = lax.broadcasted_iota(jnp.int32, (128, 128), 1)
    ridge = jnp.where(row == col, float(MEMBERS - 1), 0.0)

    def tile(h, t):
        return ff[h, :, t].reshape(128, 128)

    def right(h, first):
        keep = jnp.logical_and(col >= first, col < first + 3)
        part = jnp.sum(jnp.where(keep, tile(h, 5), 0.0), axis=1, keepdims=True)
        return jnp.broadcast_to(part, (128, 128))

    asc[...] = jnp.zeros_like(asc)
    where = {
        (0, 0): (0, 0), (0, 1): (0, 1), (0, 2): (0, 2), (0, 3): (0, 3), (3, 3): (0, 4),
        (1, 1): (1, 0), (1, 2): (1, 1), (1, 3): (1, 2), (2, 2): (1, 3), (2, 3): (1, 4),
    }
    for (i, j), (h, t) in where.items():
        block = tile(h, t)
        asc[i, :, 128 * j:128 * j + 128] = block + ridge if i == j else block
    for i, (h, first) in enumerate(((0, 0), (1, 0), (1, 64), (0, 64))):
        asc[i, :, 512:640] = right(h, first)

    def eliminate(k, carry):
        mine = pl.ds(pl.multiple_of(k * 128, 128), 128)
        w = mm(inverse(asc[k, :, mine]), asc[k])
        wsc[k] = w

        def update(i, carry):
            other = asc[k, :, pl.ds(pl.multiple_of(i * 128, 128), 128)].T
            asc[i] = asc[i] - mm(other, w)
            return carry

        lax.fori_loop(k + 1, 4, update, 0)
        return carry

    lax.fori_loop(0, 4, eliminate, 0)
    xcol[...] = jnp.zeros_like(xcol)

    def back(i, carry):
        k = 3 - i
        xcol[pl.ds(pl.multiple_of(k * 128, 128), 128), :] = wsc[k, :, 512:640] - mm(wsc[k, :, 0:512], xcol[...])
        return carry

    lax.fori_loop(0, 4, back, 0)


def kernel(
    x_ref, cc_ref, dif, vel, cells, count, value_ref, scale_ref, pred, mean_out, obs_out, mix_out,
    turn, a_buf, b_buf, coef, perm, onehot, pbf, clsf, cce, hsend, hrecv, wv, wrecv, sbuf, samples,
    fpart, rcore, rplane, zsend, zrecv, fin, ff, asc, wsc, xcol, fields, tall, line,
    s_halo, r_halo, s_cls, r_cls, s_w, r_w, s_s, r_s, s_c, r_c, s_p, r_p, s_z, r_z, s_g, r_g, s_a, r_a, s_b, r_b,
    s_f, r_f, s_o, r_o, s_l, r_l, relay,
):
    g, m = place()
    z, xl = g % 16, g // 16
    core = m % 2
    p = plane_of(g, m)
    other = m + 1 - 2 * core
    sender = g // 2 == m
    crossing = jnp.logical_or(g == 15, g == 16)
    barrier = pltpu.get_barrier_semaphore()

    def z_peer(d):
        return xl * 16 + (z + d) % 16, m

    signal(barrier, z_peer(1))
    signal(barrier, z_peer(15))

    @pl.when(crossing)
    def _():
        signal(barrier, (31 - g, m))

    def greet(d, carry):
        signal(barrier, (g, (m + d) % 16))
        signal(barrier, plane_peer((p + d) % 16, g, m))
        return carry

    lax.fori_loop(1, 16, greet, 0)

    at_row = lax.broadcasted_iota(jnp.int32, (NC, 128), 0)
    at_col = lax.broadcasted_iota(jnp.int32, (NC, 128), 1)
    for t in range(8):
        perm[:, t * 128:(t + 1) * 128] = (at_row == at_col * 8 + t).astype(F32).astype(BF16)
    both = jnp.concatenate([x_ref[...].reshape(512, NC), cc_ref[...].astype(F32).astype(BF16)], axis=0)
    for t in range(8):
        moved = jnp.dot(both, perm[:, t * 128:(t + 1) * 128], preferred_element_type=F32)
        turn[t] = moved[0:512]
        clsf[:, t * 128:(t + 1) * 128] = moved[512:528]

    def shuffle(r, carry):
        for q in range(4):
            for t in range(8):
                a_buf[q, r + HALO, :, t * 128:(t + 1) * 128] = turn[t, pl.ds(q * 128 + r, 8, stride=16), :]
        return carry

    lax.fori_loop(0, 16, shuffle, 0)
    for side in range(2):
        def pack(r, carry, side=side):
            for h in range(2):
                pair = [a_buf[2 * h + i, r + HALO + side * 10] for i in range(2)]
                hsend[side, h, r] = jnp.concatenate(pair, axis=0).astype(BF16)
            return carry

        lax.fori_loop(0, HALO, pack, 0)

    pl.semaphore_wait(barrier, 32 + crossing.astype(jnp.int32))

    def up(h):
        return remote(hsend.at[0, h], hrecv.at[1, h], s_halo.at[0, h], r_halo.at[1, h], (g - 1, m))

    def down(h):
        return remote(hsend.at[1, h], hrecv.at[0, h], s_halo.at[1, h], r_halo.at[0, h], (g + 1, m))

    cup = remote(clsf.at[pl.ds(0, 8)], cce.at[pl.ds(24, 8)], s_cls.at[0], r_cls.at[1], (g - 1, m))
    cdown = remote(clsf.at[pl.ds(8, 8)], cce.at[pl.ds(0, 8)], s_cls.at[1], r_cls.at[0], (g + 1, m))

    @pl.when(g > 0)
    def _():
        cup.start()
        up(0).start()
        up(1).start()

    @pl.when(g < 31)
    def _():
        cdown.start()
        down(0).start()
        down(1).start()

    def tell(k):
        signal(relay.at[k], z_peer(2**k))
        signal(relay.at[k], z_peer(16 - 2**k))

    tell(0)
    cce[pl.ds(8, 16), :] = clsf[...]

    @pl.when(g == 0)
    def _():
        hrecv[0] = jnp.zeros((2, HALO, 16, NC), BF16)
        cce[pl.ds(0, 8), :] = jnp.zeros((8, NC), F32)

    @pl.when(g == 31)
    def _():
        hrecv[1] = jnp.zeros((2, HALO, 16, NC), BF16)
        cce[pl.ds(24, 8), :] = jnp.zeros((8, NC), F32)

    slot = lax.broadcasted_iota(jnp.int32, (1, 128), 1)
    for s in range(32):
        valid = (slot < count[0, s]).astype(F32)
        wv[s] = jnp.concatenate([scale_ref[0, s:s + 1, :] * valid, value_ref[0, s:s + 1, :]], axis=1)
    at_place = lax.broadcasted_iota(jnp.int32, (NC, 128), 0)

    def mark(o, carry):
        spot = across(cells[0, pl.ds(o, 1), :] % NC)
        onehot[o] = (at_place == spot).astype(F32).astype(BF16)
        return carry

    lax.fori_loop(0, 32, mark, 0)
    pl.semaphore_wait(relay.at[0], 2)
    tell(1)

    @pl.when(g > 0)
    def _():
        cup.wait_send()
        cdown.wait_recv()

    @pl.when(g < 31)
    def _():
        cdown.wait_send()
        cup.wait_recv()

    fill_coefs(g, cce, dif, vel, coef)
    bufs = (a_buf, b_buf)

    def edge(src, q, r):
        return pltpu.roll(src[q, r, :, 7 * 128:], 1, 1), pltpu.roll(src[q, r, :, :128], 127, 1)

    for h in range(2):
        @pl.when(g > 0)
        def _(h=h):
            up(h).wait_send()
            down(h).wait_recv()

        @pl.when(g < 31)
        def _(h=h):
            down(h).wait_send()
            up(h).wait_recv()

        if h == 1:
            pl.semaphore_wait(relay.at[1], 2)
            tell(2)
        for side in range(2):
            def widen(r, carry, side=side, h=h):
                rows = hrecv[side, h, r].astype(F32)
                a_buf[2 * h, r + side * 22] = rows[0:8]
                a_buf[2 * h + 1, r + side * 22] = rows[8:16]
                return carry

            lax.fori_loop(0, HALO, widen, 0)
        for k in range(STEPS):
            src, dst = bufs[k % 2], bufs[(k + 1) % 2]

            def advance(r, carry, src=src, dst=dst, k=k, h=h):
                pair = []
                for q in (2 * h, 2 * h + 1):
                    mid = [src[q, r, :, t * 128:(t + 1) * 128] for t in range(8)]
                    first, last = edge(src, q, r)
                    tiles = []
                    for t in range(8):
                        lanes = slice(t * 128, (t + 1) * 128)
                        c = [jnp.broadcast_to(coef[t, r + 2, i:i + 1, :], (8, 128)) for i in range(5)]
                        left = mid[t - 1] if t else first
                        right = mid[t + 1] if t < 7 else last
                        out = c[0] * mid[t]
                        out = out + c[1] * src[q, r - 1, :, lanes] + c[2] * src[q, r + 1, :, lanes]
                        out = out + c[3] * left + c[4] * right
                        if k < STEPS - 1:
                            dst[q, r, :, lanes] = out
                        tiles.append(out)
                    pair.append(jnp.concatenate(tiles, axis=1))
                if k == STEPS - 1:
                    pbf[pl.ds((r - HALO) * 32 + 16 * h, 16), :] = jnp.concatenate(pair, axis=0).astype(BF16)
                return carry

            lax.fori_loop(k + 1, EXT - 1 - k, advance, 0, unroll=4)

    def sample(chunk):
        row = jnp.concatenate([cells[0, pl.ds(2 * chunk + i, 1), :] for i in range(2)], axis=1) // NC
        wide = jnp.dot(
            pbf[...], jnp.concatenate([onehot[2 * chunk], onehot[2 * chunk + 1]], axis=1), preferred_element_type=F32
        )
        total = jnp.zeros((32, 256), F32)
        for r in range(16):
            total = total + jnp.where(row == r, wide[r * 32:(r + 1) * 32], 0.0)
        return total.astype(BF16)

    def scatter(d, carry):
        peer = (m + d) % 16
        sbuf[d] = sample(peer)
        remote(sbuf.at[d], samples.at[m], s_s.at[d], r_s.at[m], (g, peer)).start()
        return carry

    lax.fori_loop(1, 16, scatter, 0)
    samples[m] = sample(m)

    pl.semaphore_wait(relay.at[2], 2)
    signal(relay.at[3], (g + 16 - 32 * xl, m))
    pl.semaphore_wait(relay.at[3], 1)

    @pl.when(sender)
    def _():
        def give(d, carry):
            s = (g + d) % 32
            remote(wv.at[s], wrecv.at[g % 2], s_w.at[d], r_w.at[g % 2], (s, m)).start()
            return carry

        lax.fori_loop(1, 32, give, 0)
        wrecv[g % 2] = wv[g]

    def scattered(d, carry):
        peer = (m + d) % 16
        c = remote(sbuf.at[d], samples.at[peer], s_s.at[d], r_s.at[peer], (g, peer))
        c.wait_send()
        c.wait_recv()
        return carry

    lax.fori_loop(1, 16, scattered, 0)

    @pl.when(sender)
    def _():
        def given(d, carry):
            remote(wv.at[g], wrecv.at[g % 2], s_w.at[d], r_w.at[g % 2], (g, m)).wait_send()
            return carry

        lax.fori_loop(1, 32, given, 0)

    for o in range(2):
        @pl.when(2 * m + o != g)
        def _(o=o):
            remote(wv.at[g], wrecv.at[o], s_w.at[0], r_w.at[o], (g, m)).wait_recv()

    sampled = samples[...].reshape(MEMBERS, 256).astype(F32)
    mean = jnp.sum(sampled, axis=0, keepdims=True) / MEMBERS
    weight = jnp.concatenate([wrecv[0, :, 0:128], wrecv[1, :, 0:128]], axis=1)
    value = jnp.concatenate([wrecv[0, :, 128:256], wrecv[1, :, 128:256]], axis=1)
    panel = ((sampled - mean) * weight).astype(BF16)
    parts = split3((value - mean) * weight)
    line_at = lax.broadcasted_iota(jnp.int32, (128, 256), 0)
    dep_one = jnp.zeros((128, 256), F32)
    dep_two = jnp.zeros((128, 256), F32)
    for i in range(3):
        dep_one = jnp.where(line_at == i, parts[i].astype(F32), dep_one)
        dep_two = jnp.where(line_at == 64 + i, parts[i].astype(F32), dep_two)
    dep_one = dep_one.astype(BF16)
    dep_two = dep_two.astype(BF16)
    blk = [panel[i * 128:(i + 1) * 128] for i in range(4)]

    def outer(a, b):
        return lax.dot_general(a, b, (((1,), (1,)), ((), ())), preferred_element_type=F32)

    pairs = (
        ((0, 0), (0, 1), (0, 2), (0, 3), (3, 3)),
        ((1, 1), (1, 2), (1, 3), (2, 2), (2, 3)),
    )
    for h in range(2):
        for t in range(5):
            i, j = pairs[h][t]
            fpart[h, :, t] = outer(blk[i], blk[j]).reshape(16, 8, 128)
        fpart[h, :, 5] = (outer(blk[h], dep_one) + outer(blk[3 - h], dep_two)).reshape(16, 8, 128)

    swap = remote(fpart.at[1 - core], rcore, s_c.at[0], r_c.at[0], (g, other))
    swap.start()
    swap.wait()

    def pair_sum(i, carry):
        rcore[i] = rcore[i] + fpart[core, i]
        return carry

    lax.fori_loop(0, 16, pair_sum, 0)

    def plane_give(d, carry):
        q = (p + d) % 16
        remote(rcore.at[q], rplane.at[p], s_p.at[d], r_p.at[p], plane_peer(q, g, m)).start()
        return carry

    lax.fori_loop(1, 16, plane_give, 0)

    for t in range(8):
        back = lax.dot_general(
            pbf[...], perm[t * 128:(t + 1) * 128, :], (((1,), (1,)), ((), ())), preferred_element_type=F32
        )
        for r in range(16):
            for q in range(4):
                at = r * 32 + q * 8
                turn[t, pl.ds(q * 128 + r, 8, stride=16), :] = back[at:at + 8]

    def finish(i, carry):
        for t in range(8):
            pred[i, :, t * 128:(t + 1) * 128] = turn[t, pl.ds(i * 16, 16), :].astype(BF16)
        return carry

    lax.fori_loop(0, 32, finish, 0)

    def plane_take(d, total):
        q = (p + d) % 16
        remote(rcore.at[q], rplane.at[q], s_p.at[d], r_p.at[q], plane_peer(q, g, m)).wait_recv()
        return total + rplane[q]

    zsend[...] = lax.fori_loop(1, 16, plane_take, rcore[p])

    for j in range(6):
        @pl.when(z != z_reducer(j))
        def _(j=j):
            remote(zsend.at[j], zrecv.at[z], s_z.at[j], r_z.at[z], (xl * 16 + z_reducer(j), m)).start()

    for j in range(6):
        @pl.when(z == z_reducer(j))
        def _(j=j):
            def z_take(d, total):
                q = (z + d) % 16
                remote(zsend.at[j], zrecv.at[q], s_z.at[j], r_z.at[q], (xl * 16 + q, m)).wait_recv()
                return total + zrecv[q]

            fin[p, j] = lax.fori_loop(1, 16, z_take, zsend[j])

            def z_give(d, carry):
                q = (z + d) % 16
                remote(fin.at[p, j], fin.at[p, j], s_g.at[d], r_g.at[j], (xl * 16 + q, m)).start()
                return carry

            lax.fori_loop(1, 16, z_give, 0)

    for j in range(6):
        @pl.when(z != z_reducer(j))
        def _(j=j):
            remote(fin.at[p, j], fin.at[p, j], s_g.at[0], r_g.at[j], (xl * 16 + z_reducer(j), m)).wait_recv()

    def plane_send(d, carry):
        q = (p + d) % 16
        remote(fin.at[p], fin.at[p], s_a.at[d], r_a.at[p], plane_peer(q, g, m)).start()
        return carry

    lax.fori_loop(1, 16, plane_send, 0)

    def plane_got(d, carry):
        q = (p + d) % 16
        remote(fin.at[q], fin.at[q], s_a.at[d], r_a.at[q], plane_peer(q, g, m)).wait_recv()
        return carry

    lax.fori_loop(1, 16, plane_got, 0)
    home = remote(fin, ff.at[core], s_b.at[0], r_b.at[0], (g, other))
    home.start()

    def keep(i, carry):
        ff[core, i] = fin[i]
        return carry

    lax.fori_loop(0, 16, keep, 0)
    home.wait()

    def field_give(d, carry):
        q = (m + d) % 16
        mine = pbf.at[pl.ds(pl.multiple_of(q * 32, 32), 32)]
        remote(mine, fields.at[m], s_f.at[d], r_f.at[m], (g, q)).start()
        return carry

    lax.fori_loop(1, 16, field_give, 0)
    fields[m] = pbf[pl.ds(pl.multiple_of(m * 32, 32), 32), :]
    for i in range(2):
        lanes = slice(i * 128, (i + 1) * 128)

        @pl.when(2 * m + i != g)
        def _(i=i, lanes=lanes):
            src = samples.at[:, :, lanes]
            remote(src, tall.at[g % 2], s_o.at[i], r_o.at[g % 2], (2 * m + i, g // 2)).start()

        @pl.when(2 * m + i == g)
        def _(i=i, lanes=lanes):
            tall[g % 2] = samples[:, :, lanes]

    solve(ff, asc, wsc, xcol)

    x = xcol[...]
    shift = 1.0 / MEMBERS - jnp.sum(x[:, 0:1], axis=0, keepdims=True) / MEMBERS
    coefs = []
    for k in range(4):
        piece = x[k * 128:(k + 1) * 128].T[0:8, :]
        mix_out[:, k * 128:(k + 1) * 128] = piece
        coefs.append(piece + shift)
    pieces = split3(jnp.concatenate(coefs, axis=1))

    def weigh(array):
        total = jnp.zeros((8, array.shape[1]), F32)
        for piece in pieces:
            total = total + jnp.dot(piece, array, preferred_element_type=F32)
        return total[0:1]

    def field_take(d, carry):
        q = (m + d) % 16
        mine = pbf.at[pl.ds(pl.multiple_of(q * 32, 32), 32)]
        c = remote(mine, fields.at[q], s_f.at[d], r_f.at[q], (g, q))
        c.wait_send()
        c.wait_recv()
        return carry

    lax.fori_loop(1, 16, field_take, 0)
    for i in range(2):
        @pl.when(2 * m + i != g)
        def _(i=i):
            src = samples.at[:, :, slice(0, 128)]
            remote(src, tall.at[i], s_o.at[i], r_o.at[i], (2 * m + i, g // 2)).wait_recv()
            remote(src, tall.at[i], s_o.at[i], r_o.at[i], (2 * m + i, g // 2)).wait_send()

    parts = [weigh(fields[...].reshape(MEMBERS, NC))]
    parts += [weigh(tall[i].reshape(MEMBERS, 128)) for i in range(2)]
    line[m] = jnp.concatenate(parts, axis=1)

    def line_give(d, carry):
        q = (m + d) % 16
        remote(line.at[m], line.at[m], s_l.at[d], r_l.at[m], (g, q)).start()
        return carry

    lax.fori_loop(1, 16, line_give, 0)

    def drain(d, carry):
        q = (p + d) % 16
        remote(rcore.at[q], rplane.at[q], s_p.at[d], r_p.at[q], plane_peer(q, g, m)).wait_send()
        remote(fin.at[p], fin.at[p], s_a.at[d], r_a.at[p], plane_peer(q, g, m)).wait_send()
        return carry

    lax.fori_loop(1, 16, drain, 0)
    for j in range(6):
        @pl.when(z != z_reducer(j))
        def _(j=j):
            remote(zsend.at[j], zrecv.at[z], s_z.at[j], r_z.at[z], (xl * 16 + z_reducer(j), m)).wait_send()

        @pl.when(z == z_reducer(j))
        def _(j=j):
            def z_given(d, carry):
                q = (z + d) % 16
                remote(fin.at[p, j], fin.at[p, j], s_g.at[d], r_g.at[j], (xl * 16 + q, m)).wait_send()
                return carry

            lax.fori_loop(1, 16, z_given, 0)

    def line_take(d, carry):
        q = (m + d) % 16
        c = remote(line.at[m], line.at[q], s_l.at[d], r_l.at[q], (g, q))
        c.wait_send()
        c.wait_recv()
        return carry

    lax.fori_loop(1, 16, line_take, 0)

    rows = jnp.concatenate([line[r][:, 0:NC] for r in range(16)], axis=0)
    total = jnp.zeros((16, NC), F32)
    for piece in split3(rows):
        total = total + lax.dot_general(piece, perm[...], (((1,), (1,)), ((), ())), preferred_element_type=F32)
    mean_out[...] = total
    for s in range(32):
        first = NC + (s % 2) * 128
        obs_out[s:s + 1, :] = line[s // 2][:, first:first + 128]


def local(
    prior_sample_matrix, cell_class, diffusion_table, velocity_table, obs_cells, obs_count, obs_value, obs_scale
):
    vmem = pl.BlockSpec(memory_space=pltpu.VMEM)
    smem = pl.BlockSpec(memory_space=pltpu.SMEM)
    dma = pltpu.SemaphoreType.DMA
    pred, mean, obs, mix = pl.pallas_call(
        kernel,
        out_shape=(
            jax.ShapeDtypeStruct((32, 16, NC), BF16),
            jax.ShapeDtypeStruct((16, NC), F32),
            jax.ShapeDtypeStruct((32, 128), F32),
            jax.ShapeDtypeStruct((8, MEMBERS), F32),
        ),
        in_specs=[vmem, vmem, smem, smem, vmem, smem, vmem, vmem],
        out_specs=(vmem, vmem, vmem, vmem),
        scratch_shapes=[
            pltpu.VMEM((8, 512, 128), F32),
            pltpu.VMEM((4, EXT, 8, NC), F32),
            pltpu.VMEM((4, EXT, 8, NC), F32),
            pltpu.VMEM((8, 32, 8, 128), F32),
            pltpu.VMEM((NC, NC), BF16),
            pltpu.VMEM((32, NC, 128), BF16),
            pltpu.VMEM((512, NC), BF16),
            pltpu.VMEM((16, NC), F32),
            pltpu.VMEM((32, NC), F32),
            pltpu.VMEM((2, 2, HALO, 16, NC), BF16),
            pltpu.VMEM((2, 2, HALO, 16, NC), BF16),
            pltpu.VMEM((32, 1, 256), F32),
            pltpu.VMEM((2, 1, 256), F32),
            pltpu.VMEM((16, 32, 256), BF16),
            pltpu.VMEM((16, 32, 256), BF16),
            pltpu.VMEM((2, 16, 6, 8, 128), F32),
            pltpu.VMEM((16, 6, 8, 128), F32),
            pltpu.VMEM((16, 6, 8, 128), F32),
            pltpu.VMEM((6, 8, 128), F32),
            pltpu.VMEM((16, 8, 128), F32),
            pltpu.VMEM((16, 6, 8, 128), F32),
            pltpu.VMEM((2, 16, 6, 8, 128), F32),
            pltpu.VMEM((4, 128, 640), F32),
            pltpu.VMEM((4, 128, 640), F32),
            pltpu.VMEM((MEMBERS, 128), F32),
            pltpu.VMEM((16, 32, NC), BF16),
            pltpu.VMEM((2, 16, 32, 128), BF16),
            pltpu.VMEM((16, 1, NC + 256), F32),
            dma((2, 2)), dma((2, 2)), dma((2,)), dma((2,)), dma((32,)), dma((2,)), dma((16,)), dma((16,)),
            dma((1,)), dma((1,)), dma((16,)), dma((16,)), dma((6,)), dma((16,)), dma((16,)), dma((6,)),
            dma((16,)), dma((16,)), dma((1,)), dma((1,)),
            dma((16,)), dma((16,)), dma((2,)), dma((2,)), dma((16,)), dma((16,)),
            pltpu.SemaphoreType.REGULAR((4,)),
        ],
        compiler_params=pltpu.CompilerParams(
            collective_id=0, has_side_effects=True, vmem_limit_bytes=VMEM_LIMIT
        ),
    )(prior_sample_matrix, cell_class, diffusion_table, velocity_table, obs_cells, obs_count, obs_value, obs_scale)
    return pred, mean, obs.reshape(1, 32, 128), mix[0]


def solution(mesh):
    in_specs = (
        P("member", "grid", None),
        P("grid", None),
        P(),
        P(),
        P("grid", None, None),
        P("grid", None),
        P("grid", None, None),
        P("grid", None, None),
    )
    out_specs = (P("member", "grid", None), P("grid", None), P("grid", None, None), P())
    return jax.shard_map(local, mesh=mesh, in_specs=in_specs, out_specs=out_specs, check_vma=False)
```

```python
import functools

import jax
import jax.numpy as jnp
from jax import lax
from jax.experimental import pallas as pl
from jax.experimental.pallas import tpu as pltpu
from jax.sharding import PartitionSpec as P

STEPS = 6
MEMBERS = 512
HALO = 6
EXT = 28
NC = 1024
HIGH = lax.Precision.HIGHEST
MESH = pl.DeviceIdType.MESH
F32 = jnp.float32
BF16 = jnp.bfloat16
VMEM_LIMIT = 56 * 1024 * 1024


def place():
    g = lax.axis_index("grid")
    m = lax.axis_index("member")
    return g, m


def plane_of(g, m):
    return (g // 16) * 8 + (m // 8) * 4 + (m // 2) % 4


def plane_peer(p, g, m):
    return (p // 8) * 16 + g % 16, ((p // 4) % 2) * 8 + (p % 4) * 2 + m % 2


def z_reducer(j):
    return (8 * j) // 3


def remote(src, dst, send, recv, where):
    return pltpu.make_async_remote_copy(
        src_ref=src, dst_ref=dst, send_sem=send, recv_sem=recv, device_id=where, device_id_type=MESH
    )


def signal(sem, where):
    pl.semaphore_signal(sem, inc=1, device_id=where, device_id_type=MESH)


def split3(value):
    a = value.astype(BF16)
    rest = value - a.astype(F32)
    b = rest.astype(BF16)
    c = (rest - b.astype(F32)).astype(BF16)
    return a, b, c


def across(value):
    return (value % 8) * 128 + value // 8


def fill_coefs(g, cce, dif, vel, coef):
    place_of = lax.broadcasted_iota(jnp.int32, (8, NC), 1)
    for quarter in range(4):
        rows = pl.ds(quarter * 8, 8)
        cls = cce[rows, :]
        d = jnp.zeros((8, NC), F32)
        vx = jnp.zeros((8, NC), F32)
        vy = jnp.zeros((8, NC), F32)
        for c in range(16):
            hit = cls == float(c)
            d = jnp.where(hit, dif[c], d)
            vx = jnp.where(hit, vel[0, c], vx)
            vy = jnp.where(hit, vel[1, c], vy)
        row = lax.broadcasted_iota(jnp.int32, (8, NC), 0) + (quarter * 8 - 8) + g * 16
        inside = jnp.logical_and(row >= 0, row < 512)
        values = (
            jnp.where(inside, 1.0 - 4.0 * d, 0.0),
            jnp.where(inside, d + 0.5 * vy, 0.0),
            jnp.where(inside, d - 0.5 * vy, 0.0),
            jnp.where(jnp.logical_and(inside, place_of > 0), d + 0.5 * vx, 0.0),
            jnp.where(jnp.logical_and(inside, place_of < NC - 1), d - 0.5 * vx, 0.0),
        )
        for i in range(5):
            for t in range(8):
                coef[t, quarter * 8:quarter * 8 + 8, i, :] = values[i][:, t * 128:(t + 1) * 128]


def inverse(a):
    lane = lax.broadcasted_iota(jnp.int32, (8, 128), 1)
    line = lax.broadcasted_iota(jnp.int32, (8, 128), 0)
    v = [a[8 * i:8 * i + 8] for i in range(16)]

    def column(i, t, j):
        return jnp.broadcast_to(v[i][:, 8 * t + j:8 * t + j + 1], (8, 128))

    for t in range(16):
        inside = jnp.logical_and(lane >= 8 * t, lane < 8 * t + 8)
        u = jnp.where(inside, (lane - 8 * t == line).astype(F32), v[t])
        k = [column(t, t, j) for j in range(8)]
        for s in range(8):
            inv = 1.0 / k[s][s:s + 1]
            here = line == s
            for j in range(s + 1, 8):
                r = k[j][s:s + 1] * inv
                k[j] = jnp.where(here, r, k[j] - k[s] * r)
            r = u[s:s + 1] * inv
            u = jnp.where(here, r, u - k[s] * r)
        others = [(t + d) % 16 for d in range(1, 16)]
        col = [{i: column(i, t, j) for i in others} for j in range(8)]
        rows = [jnp.broadcast_to(u[s:s + 1], (8, 128)) for s in range(8)]
        for i in others:
            w = jnp.where(inside, 0.0, v[i])
            x0 = col[0][i] * rows[0] + col[1][i] * rows[1]
            x1 = col[2][i] * rows[2] + col[3][i] * rows[3]
            x2 = col[4][i] * rows[4] + col[5][i] * rows[5]
            x3 = col[6][i] * rows[6] + col[7][i] * rows[7]
            v[i] = w - ((x0 + x1) + (x2 + x3))
        v[t] = u
    return jnp.concatenate(v, axis=0)


def mm(a, b):
    return jnp.dot(a, b, precision=HIGH, preferred_element_type=F32)


def solve(ff, asc, wsc, inv, xcol):
    row = lax.broadcasted_iota(jnp.int32, (128, 128), 0)
    col = lax.broadcasted_iota(jnp.int32, (128, 128), 1)
    ridge = jnp.where(row == col, float(MEMBERS - 1), 0.0)

    def tile(h, t):
        return ff[h, :, t].reshape(128, 128)

    def right(h, first):
        keep = jnp.logical_and(col >= first, col < first + 3)
        part = jnp.sum(jnp.where(keep, tile(h, 5), 0.0), axis=1, keepdims=True)
        return jnp.broadcast_to(part, (128, 128))

    where = {
        (0, 0): (0, 0), (0, 1): (0, 1), (0, 2): (0, 2), (0, 3): (0, 3), (3, 3): (0, 4),
        (1, 1): (1, 0), (1, 2): (1, 1), (1, 3): (1, 2), (2, 2): (1, 3), (2, 3): (1, 4),
    }
    for (i, j), (h, t) in where.items():
        block = tile(h, t)
        asc[i, :, 128 * j:128 * j + 128] = block + ridge if i == j else block
    for i, (h, first) in enumerate(((0, 0), (1, 0), (1, 64), (0, 64))):
        asc[i, :, 512:640] = right(h, first)

    def eliminate(k, carry):
        inv[...] = inverse(asc[k, :, pl.ds(pl.multiple_of(k * 128, 128), 128)])
        for n in range(4):
            @pl.when(k == n)
            def _(n=n):
                w = mm(inv[...], asc[n, :, 128 * n + 128:640])
                wsc[n, :, 128 * n + 128:640] = w
                for i in range(n + 1, 4):
                    other = asc[n, :, 128 * i:128 * i + 128].T
                    asc[i, :, 128 * i:640] = asc[i, :, 128 * i:640] - mm(other, w[:, 128 * (i - n - 1):])
        return carry

    lax.fori_loop(0, 4, eliminate, 0)
    for k in reversed(range(4)):
        y = wsc[k, :, 512:640]
        if k < 3:
            y = y - mm(wsc[k, :, 128 * k + 128:512], xcol[128 * k + 128:512, :])
        xcol[128 * k:128 * k + 128, :] = y


def kernel(
    x_hbm, cc_hbm, dif, vel, cells_hbm, count, value_hbm, scale_hbm, pred_hbm, mean_hbm, obs_hbm, mix_hbm,
    x_ref, cc_ref, cells, value_ref, scale_ref, pred, mean_out, obs_out, mix_out, s_in, s_out,
    turn, a_buf, b_buf, coef, perm, onehot, pbf, clsf, cce, hsend, hrecv, wv, wrecv, sbuf, samples,
    fpart, rcore, rplane, zsend, zrecv, fin, ff, asc, wsc, inv, xcol, fields, osend, orecv, line,
    s_halo, r_halo, s_cls, r_cls, s_w, r_w, s_s, r_s, s_c, r_c, s_p, r_p, s_z, r_z, s_g, r_g, s_a, r_a, s_b, r_b,
    s_f, r_f, s_o, r_o, s_l, r_l, relay,
):
    g, m = place()
    z, xl = g % 16, g // 16
    core = m % 2
    p = plane_of(g, m)
    other = m + 1 - 2 * core
    sender = g // 2 == m
    crossing = jnp.logical_or(g == 15, g == 16)
    barrier = pltpu.get_barrier_semaphore()

    def z_peer(d):
        return xl * 16 + (z + d) % 16, m

    arrays = ((x_hbm, x_ref), (cc_hbm, cc_ref), (cells_hbm, cells), (value_hbm, value_ref), (scale_hbm, scale_ref))
    loads = [pltpu.make_async_copy(a, b, s_in.at[i]) for i, (a, b) in enumerate(arrays)]
    for load in loads:
        load.start()
    arrays = ((pred, pred_hbm), (mean_out, mean_hbm), (obs_out, obs_hbm), (mix_out, mix_hbm))
    stores = [pltpu.make_async_copy(a, b, s_out.at[i]) for i, (a, b) in enumerate(arrays)]

    signal(barrier, z_peer(1))
    signal(barrier, z_peer(15))

    @pl.when(crossing)
    def _():
        signal(barrier, (31 - g, m))

    def greet(d, carry):
        signal(barrier, (g, (m + d) % 16))
        signal(barrier, plane_peer((p + d) % 16, g, m))
        return carry

    lax.fori_loop(1, 16, greet, 0)

    at_row = lax.broadcasted_iota(jnp.int32, (NC, 128), 0)
    at_col = lax.broadcasted_iota(jnp.int32, (NC, 128), 1)
    for t in range(8):
        perm[:, t * 128:(t + 1) * 128] = (at_row == at_col * 8 + t).astype(F32).astype(BF16)
    loads[0].wait()
    loads[1].wait()
    both = jnp.concatenate([x_ref[...].reshape(512, NC), cc_ref[...].astype(F32).astype(BF16)], axis=0)
    for t in range(8):
        moved = jnp.dot(both, perm[:, t * 128:(t + 1) * 128], preferred_element_type=F32)
        turn[t] = moved[0:512]
        clsf[:, t * 128:(t + 1) * 128] = moved[512:528]

    def shuffle(r, carry):
        for q in range(4):
            for t in range(8):
                a_buf[q, r + HALO, :, t * 128:(t + 1) * 128] = turn[t, pl.ds(q * 128 + r, 8, stride=16), :]
        return carry

    lax.fori_loop(0, 16, shuffle, 0)
    for side in range(2):
        def pack(r, carry, side=side):
            for h in range(2):
                pair = [a_buf[2 * h + i, r + HALO + side * 10] for i in range(2)]
                hsend[side, h, r] = jnp.concatenate(pair, axis=0).astype(BF16)
            return carry

        lax.fori_loop(0, HALO, pack, 0)

    pl.semaphore_wait(barrier, 32 + crossing.astype(jnp.int32))

    def up(h):
        return remote(hsend.at[0, h], hrecv.at[1, h], s_halo.at[0, h], r_halo.at[1, h], (g - 1, m))

    def down(h):
        return remote(hsend.at[1, h], hrecv.at[0, h], s_halo.at[1, h], r_halo.at[0, h], (g + 1, m))

    cup = remote(clsf.at[pl.ds(0, 8)], cce.at[pl.ds(24, 8)], s_cls.at[0], r_cls.at[1], (g - 1, m))
    cdown = remote(clsf.at[pl.ds(8, 8)], cce.at[pl.ds(0, 8)], s_cls.at[1], r_cls.at[0], (g + 1, m))

    @pl.when(g > 0)
    def _():
        cup.start()
        up(0).start()

    @pl.when(g < 31)
    def _():
        cdown.start()
        down(0).start()

    def tell(k):
        signal(relay.at[k], z_peer(2**k))
        signal(relay.at[k], z_peer(16 - 2**k))

    tell(0)
    cce[pl.ds(8, 16), :] = clsf[...]

    @pl.when(g == 0)
    def _():
        hrecv[0] = jnp.zeros((2, HALO, 16, NC), BF16)
        cce[pl.ds(0, 8), :] = jnp.zeros((8, NC), F32)

    @pl.when(g == 31)
    def _():
        hrecv[1] = jnp.zeros((2, HALO, 16, NC), BF16)
        cce[pl.ds(24, 8), :] = jnp.zeros((8, NC), F32)

    for load in loads[2:]:
        load.wait()
    slot = lax.broadcasted_iota(jnp.int32, (1, 128), 1)
    for s in range(32):
        valid = (slot < count[0, s]).astype(F32)
        wv[s] = jnp.concatenate([scale_ref[0, s:s + 1, :] * valid, value_ref[0, s:s + 1, :]], axis=1)
    at_place = lax.broadcasted_iota(jnp.int32, (NC, 128), 0)

    def mark(o, carry):
        spot = across(cells[0, pl.ds(o, 1), :] % NC)
        onehot[o] = (at_place == spot).astype(F32).astype(BF16)
        return carry

    lax.fori_loop(0, 32, mark, 0)

    @pl.when(g > 0)
    def _():
        up(1).start()
        cup.wait_send()
        cdown.wait_recv()

    @pl.when(g < 31)
    def _():
        down(1).start()
        cdown.wait_send()
        cup.wait_recv()

    pl.semaphore_wait(relay.at[0], 2)
    tell(1)

    fill_coefs(g, cce, dif, vel, coef)
    bufs = (a_buf, b_buf)

    def edge(src, q, r):
        return pltpu.roll(src[q, r, :, 7 * 128:], 1, 1), pltpu.roll(src[q, r, :, :128], 127, 1)

    def give_weights():
        @pl.when(sender)
        def _():
            def give(d, carry):
                s = (g + d) % 32
                remote(wv.at[s], wrecv.at[g % 2], s_w.at[d], r_w.at[g % 2], (s, m)).start()
                return carry

            lax.fori_loop(1, 32, give, 0)
            wrecv[g % 2] = wv[g]

    for h in range(2):
        @pl.when(g > 0)
        def _(h=h):
            up(h).wait_send()
            down(h).wait_recv()

        @pl.when(g < 31)
        def _(h=h):
            down(h).wait_send()
            up(h).wait_recv()

        for side in range(2):
            def widen(r, carry, side=side, h=h):
                rows = hrecv[side, h, r].astype(F32)
                a_buf[2 * h, r + side * 22] = rows[0:8]
                a_buf[2 * h + 1, r + side * 22] = rows[8:16]
                return carry

            lax.fori_loop(0, HALO, widen, 0)
        for k in range(STEPS):
            src, dst = bufs[k % 2], bufs[(k + 1) % 2]

            def advance(r, carry, src=src, dst=dst, k=k, h=h):
                pair = []
                for q in (2 * h, 2 * h + 1):
                    mid = [src[q, r, :, t * 128:(t + 1) * 128] for t in range(8)]
                    first, last = edge(src, q, r)
                    tiles = []
                    for t in range(8):
                        lanes = slice(t * 128, (t + 1) * 128)
                        c = [jnp.broadcast_to(coef[t, r + 2, i:i + 1, :], (8, 128)) for i in range(5)]
                        left = mid[t - 1] if t else first
                        right = mid[t + 1] if t < 7 else last
                        out = c[0] * mid[t]
                        out = out + c[1] * src[q, r - 1, :, lanes] + c[2] * src[q, r + 1, :, lanes]
                        out = out + c[3] * left + c[4] * right
                        if k < STEPS - 1:
                            dst[q, r, :, lanes] = out
                        tiles.append(out)
                    pair.append(jnp.concatenate(tiles, axis=1))
                if k == STEPS - 1:
                    pbf[pl.ds((r - HALO) * 32 + 16 * h, 16), :] = jnp.concatenate(pair, axis=0).astype(BF16)
                return carry

            lax.fori_loop(k + 1, EXT - 1 - k, advance, 0, unroll=4)
            if (h, k) == (0, 0):
                pl.semaphore_wait(relay.at[1], 2)
                tell(2)
            if (h, k) == (0, 4):
                pl.semaphore_wait(relay.at[2], 2)
                signal(relay.at[3], (g + 16 - 32 * xl, m))
            if (h, k) == (1, 2):
                pl.semaphore_wait(relay.at[3], 1)
                give_weights()

    def sample(chunk):
        row = jnp.concatenate([cells[0, pl.ds(2 * chunk + i, 1), :] for i in range(2)], axis=1) // NC
        wide = jnp.dot(
            pbf[...], jnp.concatenate([onehot[2 * chunk], onehot[2 * chunk + 1]], axis=1), preferred_element_type=F32
        )
        total = jnp.zeros((32, 256), F32)
        for r in range(16):
            total = total + jnp.where(row == r, wide[r * 32:(r + 1) * 32], 0.0)
        return total.astype(BF16)

    def scatter(e, carry):
        k = (e // 2) % 4
        step = jnp.where(k < 2, 2 + k, 3 - k)
        peer = ((m // 8 + 1 - e // 8) % 2) * 8 + ((m // 2 + step) % 4) * 2 + (m + 1 + e) % 2
        sbuf[peer] = sample(peer)
        remote(sbuf.at[peer], samples.at[m], s_s.at[peer], r_s.at[m], (g, peer)).start()
        return carry

    lax.fori_loop(0, 15, scatter, 0)
    samples[m] = sample(m)

    def scattered(d, carry):
        peer = (m + d) % 16
        c = remote(sbuf.at[peer], samples.at[peer], s_s.at[peer], r_s.at[peer], (g, peer))
        c.wait_send()
        c.wait_recv()
        return carry

    lax.fori_loop(1, 16, scattered, 0)

    @pl.when(sender)
    def _():
        def given(d, carry):
            remote(wv.at[g], wrecv.at[g % 2], s_w.at[d], r_w.at[g % 2], (g, m)).wait_send()
            return carry

        lax.fori_loop(1, 32, given, 0)

    for o in range(2):
        @pl.when(2 * m + o != g)
        def _(o=o):
            remote(wv.at[g], wrecv.at[o], s_w.at[0], r_w.at[o], (g, m)).wait_recv()

    sampled = samples[...].reshape(MEMBERS, 256).astype(F32)
    mean = jnp.sum(sampled, axis=0, keepdims=True) / MEMBERS
    weight = jnp.concatenate([wrecv[0, :, 0:128], wrecv[1, :, 0:128]], axis=1)
    value = jnp.concatenate([wrecv[0, :, 128:256], wrecv[1, :, 128:256]], axis=1)
    panel = ((sampled - mean) * weight).astype(BF16)
    parts = split3((value - mean) * weight)
    line_at = lax.broadcasted_iota(jnp.int32, (128, 256), 0)
    dep_one = jnp.zeros((128, 256), F32)
    dep_two = jnp.zeros((128, 256), F32)
    for i in range(3):
        dep_one = jnp.where(line_at == i, parts[i].astype(F32), dep_one)
        dep_two = jnp.where(line_at == 64 + i, parts[i].astype(F32), dep_two)
    dep_one = dep_one.astype(BF16)
    dep_two = dep_two.astype(BF16)
    blk = [panel[i * 128:(i + 1) * 128] for i in range(4)]

    def outer(a, b):
        return lax.dot_general(a, b, (((1,), (1,)), ((), ())), preferred_element_type=F32)

    pairs = (
        ((0, 0), (0, 1), (0, 2), (0, 3), (3, 3)),
        ((1, 1), (1, 2), (1, 3), (2, 2), (2, 3)),
    )
    for h in range(2):
        for t in range(5):
            i, j = pairs[h][t]
            fpart[h, :, t] = outer(blk[i], blk[j]).reshape(16, 8, 128)
        fpart[h, :, 5] = (outer(blk[h], dep_one) + outer(blk[3 - h], dep_two)).reshape(16, 8, 128)

    swap = remote(fpart.at[1 - core], rcore, s_c.at[0], r_c.at[0], (g, other))
    swap.start()
    swap.wait()

    def pair_sum(i, carry):
        rcore[i] = rcore[i] + fpart[core, i]
        return carry

    lax.fori_loop(0, 16, pair_sum, 0)

    def plane_give(d, carry):
        q = (p + d) % 16
        remote(rcore.at[q], rplane.at[p], s_p.at[d], r_p.at[p], plane_peer(q, g, m)).start()
        return carry

    lax.fori_loop(1, 16, plane_give, 0)

    for t in range(8):
        back = lax.dot_general(
            pbf[...], perm[t * 128:(t + 1) * 128, :], (((1,), (1,)), ((), ())), preferred_element_type=F32
        )
        for r in range(16):
            for q in range(4):
                at = r * 32 + q * 8
                turn[t, pl.ds(q * 128 + r, 8, stride=16), :] = back[at:at + 8]

    def finish(i, carry):
        for t in range(8):
            pred[i, :, t * 128:(t + 1) * 128] = turn[t, pl.ds(i * 16, 16), :].astype(BF16)
        return carry

    lax.fori_loop(0, 32, finish, 0)
    stores[0].start()

    def plane_take(d, total):
        q = (p + d) % 16
        remote(rcore.at[q], rplane.at[q], s_p.at[d], r_p.at[q], plane_peer(q, g, m)).wait_recv()
        return total + rplane[q]

    zsend[...] = lax.fori_loop(1, 16, plane_take, rcore[p])

    def field_give(d, carry):
        q = (m + d) % 16
        mine = pbf.at[pl.ds(pl.multiple_of(q * 32, 32), 32)]
        remote(mine, fields.at[m], s_f.at[d], r_f.at[m], (g, q)).start()
        return carry

    lax.fori_loop(1, 16, field_give, 0)
    fields[m] = pbf[pl.ds(pl.multiple_of(m * 32, 32), 32), :]
    for j in range(6):
        @pl.when(z != z_reducer(j))
        def _(j=j):
            remote(zsend.at[j], zrecv.at[z], s_z.at[j], r_z.at[z], (xl * 16 + z_reducer(j), m)).start()

    for j in range(6):
        @pl.when(z == z_reducer(j))
        def _(j=j):
            def z_take(d, total):
                q = (z + d) % 16
                remote(zsend.at[j], zrecv.at[q], s_z.at[j], r_z.at[q], (xl * 16 + q, m)).wait_recv()
                return total + zrecv[q]

            fin[p, j] = lax.fori_loop(1, 16, z_take, zsend[j])

            def z_give(d, carry):
                q = (z + d) % 16
                remote(fin.at[p, j], fin.at[p, j], s_g.at[d], r_g.at[j], (xl * 16 + q, m)).start()
                return carry

            lax.fori_loop(1, 16, z_give, 0)

    for j in range(6):
        @pl.when(z != z_reducer(j))
        def _(j=j):
            remote(fin.at[p, j], fin.at[p, j], s_g.at[0], r_g.at[j], (xl * 16 + z_reducer(j), m)).wait_recv()

    def plane_send(d, carry):
        q = (p + d) % 16
        remote(fin.at[p], fin.at[p], s_a.at[d], r_a.at[p], plane_peer(q, g, m)).start()
        return carry

    lax.fori_loop(1, 16, plane_send, 0)

    def home(q):
        return remote(fin.at[q], ff.at[core, q], s_b.at[q], r_b.at[q], (g, other))

    home(p).start()
    ff[core, p] = fin[p]

    def plane_got(d, carry):
        q = (p + d) % 16
        remote(fin.at[q], fin.at[q], s_a.at[d], r_a.at[q], plane_peer(q, g, m)).wait_recv()
        home(q).start()
        ff[core, q] = fin[q]
        return carry

    lax.fori_loop(1, 16, plane_got, 0)

    def homed(q, carry):
        home(q).wait_send()
        remote(fin.at[q], ff.at[1 - core, q], s_b.at[q], r_b.at[q], (g, other)).wait_recv()
        return carry

    lax.fori_loop(0, 16, homed, 0)

    solve(ff, asc, wsc, inv, xcol)

    x = xcol[...]
    shift = 1.0 / MEMBERS - jnp.sum(x[:, 0:1], axis=0, keepdims=True) / MEMBERS
    coefs = []
    for k in range(4):
        piece = x[k * 128:(k + 1) * 128].T[0:8, :]
        mix_out[:, k * 128:(k + 1) * 128] = piece[0:1]
        coefs.append(piece + shift)
    pieces = split3(jnp.concatenate(coefs, axis=1))

    def weigh(array):
        total = jnp.zeros((8, array.shape[1]), F32)
        for piece in pieces:
            total = total + jnp.dot(piece, array, preferred_element_type=F32)
        return total[0:1]

    slots = weigh(samples[...].reshape(MEMBERS, 256))
    osend[0] = slots[:, 0:128]
    osend[1] = slots[:, 128:256]

    def show(d, carry):
        o = 2 * m + d // 16
        q = d % 16

        @pl.when(jnp.logical_or(o != g, q != m))
        def _():
            remote(osend.at[d // 16], orecv.at[g], s_o.at[d], r_o.at[g], (o, q)).start()

        @pl.when(jnp.logical_and(o == g, q == m))
        def _():
            orecv[g] = osend[d // 16]
        return carry

    lax.fori_loop(0, 32, show, 0)

    def field_take(d, carry):
        q = (m + d) % 16
        mine = pbf.at[pl.ds(pl.multiple_of(q * 32, 32), 32)]
        c = remote(mine, fields.at[q], s_f.at[d], r_f.at[q], (g, q))
        c.wait_send()
        c.wait_recv()
        return carry

    lax.fori_loop(1, 16, field_take, 0)
    line[m] = weigh(fields[...].reshape(MEMBERS, NC))

    def line_give(d, carry):
        q = (m + d) % 16
        remote(line.at[m], line.at[m], s_l.at[d], r_l.at[m], (g, q)).start()
        return carry

    lax.fori_loop(1, 16, line_give, 0)

    def drain(d, carry):
        q = (p + d) % 16
        remote(rcore.at[q], rplane.at[q], s_p.at[d], r_p.at[q], plane_peer(q, g, m)).wait_send()
        remote(fin.at[p], fin.at[p], s_a.at[d], r_a.at[p], plane_peer(q, g, m)).wait_send()
        return carry

    lax.fori_loop(1, 16, drain, 0)
    for j in range(6):
        @pl.when(z != z_reducer(j))
        def _(j=j):
            remote(zsend.at[j], zrecv.at[z], s_z.at[j], r_z.at[z], (xl * 16 + z_reducer(j), m)).wait_send()

        @pl.when(z == z_reducer(j))
        def _(j=j):
            def z_given(d, carry):
                q = (z + d) % 16
                remote(fin.at[p, j], fin.at[p, j], s_g.at[d], r_g.at[j], (xl * 16 + q, m)).wait_send()
                return carry

            lax.fori_loop(1, 16, z_given, 0)

    def line_take(d, carry):
        q = (m + d) % 16
        c = remote(line.at[m], line.at[q], s_l.at[d], r_l.at[q], (g, q))
        c.wait_send()
        c.wait_recv()
        return carry

    lax.fori_loop(1, 16, line_take, 0)

    rows = jnp.concatenate([line[r] for r in range(16)], axis=0)
    total = jnp.zeros((16, NC), F32)
    for piece in split3(rows):
        total = total + lax.dot_general(piece, perm[...], (((1,), (1,)), ((), ())), preferred_element_type=F32)
    mean_out[...] = total

    def seen(s, carry):
        @pl.when(jnp.logical_or(s != g, m != g // 2))
        def _():
            remote(osend.at[0], orecv.at[s], s_o.at[0], r_o.at[s], (s, g // 2)).wait_recv()
        return carry

    lax.fori_loop(0, 32, seen, 0)
    for s in range(32):
        obs_out[s:s + 1, :] = orecv[s]
    for store in stores[1:]:
        store.start()

    def shown(d, carry):
        o = 2 * m + d // 16
        q = d % 16

        @pl.when(jnp.logical_or(o != g, q != m))
        def _():
            remote(osend.at[d // 16], orecv.at[g], s_o.at[d], r_o.at[g], (o, q)).wait_send()
        return carry

    lax.fori_loop(0, 32, shown, 0)
    for store in stores:
        store.wait()


def local(
    prior_sample_matrix, cell_class, diffusion_table, velocity_table, obs_cells, obs_count, obs_value, obs_scale
):
    hbm = pl.BlockSpec(memory_space=pl.ANY)
    smem = pl.BlockSpec(memory_space=pltpu.SMEM)
    dma = pltpu.SemaphoreType.DMA
    pred, mean, obs, mix = pl.pallas_call(
        kernel,
        out_shape=(
            jax.ShapeDtypeStruct((32, 16, NC), BF16),
            jax.ShapeDtypeStruct((16, NC), F32),
            jax.ShapeDtypeStruct((32, 128), F32),
            jax.ShapeDtypeStruct((1, MEMBERS), F32),
        ),
        in_specs=[hbm, hbm, smem, smem, hbm, smem, hbm, hbm],
        out_specs=(hbm, hbm, hbm, hbm),
        scratch_shapes=[
            pltpu.VMEM((32, 16, NC), BF16),
            pltpu.VMEM((16, NC), jnp.int32),
            pltpu.VMEM((1, 32, 128), jnp.int32),
            pltpu.VMEM((1, 32, 128), F32),
            pltpu.VMEM((1, 32, 128), F32),
            pltpu.VMEM((32, 16, NC), BF16),
            pltpu.VMEM((16, NC), F32),
            pltpu.VMEM((32, 128), F32),
            pltpu.VMEM((1, MEMBERS), F32),
            dma((5,)),
            dma((4,)),
            pltpu.VMEM((8, 512, 128), F32),
            pltpu.VMEM((4, EXT, 8, NC), F32),
            pltpu.VMEM((4, EXT, 8, NC), F32),
            pltpu.VMEM((8, 32, 8, 128), F32),
            pltpu.VMEM((NC, NC), BF16),
            pltpu.VMEM((32, NC, 128), BF16),
            pltpu.VMEM((512, NC), BF16),
            pltpu.VMEM((16, NC), F32),
            pltpu.VMEM((32, NC), F32),
            pltpu.VMEM((2, 2, HALO, 16, NC), BF16),
            pltpu.VMEM((2, 2, HALO, 16, NC), BF16),
            pltpu.VMEM((32, 1, 256), F32),
            pltpu.VMEM((2, 1, 256), F32),
            pltpu.VMEM((16, 32, 256), BF16),
            pltpu.VMEM((16, 32, 256), BF16),
            pltpu.VMEM((2, 16, 6, 8, 128), F32),
            pltpu.VMEM((16, 6, 8, 128), F32),
            pltpu.VMEM((16, 6, 8, 128), F32),
            pltpu.VMEM((6, 8, 128), F32),
            pltpu.VMEM((16, 8, 128), F32),
            pltpu.VMEM((16, 6, 8, 128), F32),
            pltpu.VMEM((2, 16, 6, 8, 128), F32),
            pltpu.VMEM((4, 128, 640), F32),
            pltpu.VMEM((4, 128, 640), F32),
            pltpu.VMEM((128, 128), F32),
            pltpu.VMEM((MEMBERS, 128), F32),
            pltpu.VMEM((16, 32, NC), BF16),
            pltpu.VMEM((2, 1, 128), F32),
            pltpu.VMEM((32, 1, 128), F32),
            pltpu.VMEM((16, 1, NC), F32),
            dma((2, 2)), dma((2, 2)), dma((2,)), dma((2,)), dma((32,)), dma((2,)), dma((16,)), dma((16,)),
            dma((1,)), dma((1,)), dma((16,)), dma((16,)), dma((6,)), dma((16,)), dma((16,)), dma((6,)),
            dma((16,)), dma((16,)), dma((16,)), dma((16,)),
            dma((16,)), dma((16,)), dma((32,)), dma((32,)), dma((16,)), dma((16,)),
            pltpu.SemaphoreType.REGULAR((4,)),
        ],
        compiler_params=pltpu.CompilerParams(
            collective_id=0, has_side_effects=True, vmem_limit_bytes=VMEM_LIMIT
        ),
    )(prior_sample_matrix, cell_class, diffusion_table, velocity_table, obs_cells, obs_count, obs_value, obs_scale)
    return pred, mean, obs.reshape(1, 32, 128), mix.reshape(MEMBERS)


def solution(mesh):
    in_specs = (
        P("member", "grid", None),
        P("grid", None),
        P(),
        P(),
        P("grid", None, None),
        P("grid", None),
        P("grid", None, None),
        P("grid", None, None),
    )
    out_specs = (P("member", "grid", None), P("grid", None), P("grid", None, None), P())
    return jax.shard_map(local, mesh=mesh, in_specs=in_specs, out_specs=out_specs, check_vma=False)
```

```python
import functools

import jax
import jax.numpy as jnp
from jax import lax
from jax.experimental import pallas as pl
from jax.experimental.pallas import tpu as pltpu
from jax.sharding import PartitionSpec as P

STEPS = 6
MEMBERS = 512
HALO = 6
EXT = 28
NC = 1024
HIGH = lax.Precision.HIGHEST
MESH = pl.DeviceIdType.MESH
F32 = jnp.float32
BF16 = jnp.bfloat16
VMEM_LIMIT = 56 * 1024 * 1024


def place():
    g = lax.axis_index("grid")
    m = lax.axis_index("member")
    return g, m


def plane_of(g, m):
    return (g // 16) * 8 + (m // 8) * 4 + (m // 2) % 4


def plane_peer(p, g, m):
    return (p // 8) * 16 + g % 16, ((p // 4) % 2) * 8 + (p % 4) * 2 + m % 2


def z_reducer(j):
    return (8 * j) // 3


def remote(src, dst, send, recv, where):
    return pltpu.make_async_remote_copy(
        src_ref=src, dst_ref=dst, send_sem=send, recv_sem=recv, device_id=where, device_id_type=MESH
    )


def signal(sem, where):
    pl.semaphore_signal(sem, inc=1, device_id=where, device_id_type=MESH)


def split3(value):
    a = value.astype(BF16)
    rest = value - a.astype(F32)
    b = rest.astype(BF16)
    c = (rest - b.astype(F32)).astype(BF16)
    return a, b, c


def across(value):
    return (value % 8) * 128 + value // 8


def fill_coefs(quarters, g, cce, dif, vel, coef):
    place_of = lax.broadcasted_iota(jnp.int32, (8, NC), 1)
    for quarter in quarters:
        rows = pl.ds(quarter * 8, 8)
        cls = cce[rows, :]
        d = jnp.zeros((8, NC), F32)
        vx = jnp.zeros((8, NC), F32)
        vy = jnp.zeros((8, NC), F32)
        for c in range(16):
            hit = cls == float(c)
            d = jnp.where(hit, dif[c], d)
            vx = jnp.where(hit, vel[0, c], vx)
            vy = jnp.where(hit, vel[1, c], vy)
        row = lax.broadcasted_iota(jnp.int32, (8, NC), 0) + (quarter * 8 - 8) + g * 16
        inside = jnp.logical_and(row >= 0, row < 512)
        values = (
            jnp.where(inside, 1.0 - 4.0 * d, 0.0),
            jnp.where(inside, d + 0.5 * vy, 0.0),
            jnp.where(inside, d - 0.5 * vy, 0.0),
            jnp.where(jnp.logical_and(inside, place_of > 0), d + 0.5 * vx, 0.0),
            jnp.where(jnp.logical_and(inside, place_of < NC - 1), d - 0.5 * vx, 0.0),
        )
        for i in range(5):
            for t in range(8):
                coef[t, quarter * 8:quarter * 8 + 8, i, :] = values[i][:, t * 128:(t + 1) * 128]


def inverse(a):
    lane = lax.broadcasted_iota(jnp.int32, (8, 128), 1)
    line = lax.broadcasted_iota(jnp.int32, (8, 128), 0)
    v = [a[8 * i:8 * i + 8] for i in range(16)]

    def column(i, t, j):
        return jnp.broadcast_to(v[i][:, 8 * t + j:8 * t + j + 1], (8, 128))

    for t in range(16):
        inside = jnp.logical_and(lane >= 8 * t, lane < 8 * t + 8)
        u = jnp.where(inside, (lane - 8 * t == line).astype(F32), v[t])
        k = [column(t, t, j) for j in range(8)]
        for s in range(8):
            inv = 1.0 / k[s][s:s + 1]
            here = line == s
            for j in range(s + 1, 8):
                r = k[j][s:s + 1] * inv
                k[j] = jnp.where(here, r, k[j] - k[s] * r)
            r = u[s:s + 1] * inv
            u = jnp.where(here, r, u - k[s] * r)
        others = [(t + d) % 16 for d in range(1, 16)]
        col = [{i: column(i, t, j) for i in others} for j in range(8)]
        rows = [jnp.broadcast_to(u[s:s + 1], (8, 128)) for s in range(8)]
        for i in others:
            w = jnp.where(inside, 0.0, v[i])
            x0 = col[0][i] * rows[0] + col[1][i] * rows[1]
            x1 = col[2][i] * rows[2] + col[3][i] * rows[3]
            x2 = col[4][i] * rows[4] + col[5][i] * rows[5]
            x3 = col[6][i] * rows[6] + col[7][i] * rows[7]
            v[i] = w - ((x0 + x1) + (x2 + x3))
        v[t] = u
    return jnp.concatenate(v, axis=0)


def mm(a, b):
    return jnp.dot(a, b, precision=HIGH, preferred_element_type=F32)


def solve(ff, asc, wsc, inv, xcol):
    row = lax.broadcasted_iota(jnp.int32, (128, 128), 0)
    col = lax.broadcasted_iota(jnp.int32, (128, 128), 1)
    ridge = jnp.where(row == col, float(MEMBERS - 1), 0.0)

    def tile(h, t):
        return ff[h, :, t].reshape(128, 128)

    def right(h, first):
        keep = jnp.logical_and(col >= first, col < first + 3)
        part = jnp.sum(jnp.where(keep, tile(h, 5), 0.0), axis=1, keepdims=True)
        return jnp.broadcast_to(part, (128, 128))

    where = {
        (0, 0): (0, 0), (0, 1): (0, 1), (0, 2): (0, 2), (0, 3): (0, 3), (3, 3): (0, 4),
        (1, 1): (1, 0), (1, 2): (1, 1), (1, 3): (1, 2), (2, 2): (1, 3), (2, 3): (1, 4),
    }
    for (i, j), (h, t) in where.items():
        block = tile(h, t)
        asc[i, :, 128 * j:128 * j + 128] = block + ridge if i == j else block
    for i, (h, first) in enumerate(((0, 0), (1, 0), (1, 64), (0, 64))):
        asc[i, :, 512:640] = right(h, first)

    def eliminate(k, carry):
        inv[...] = inverse(asc[k, :, pl.ds(pl.multiple_of(k * 128, 128), 128)])
        for n in range(4):
            @pl.when(k == n)
            def _(n=n):
                w = mm(inv[...], asc[n, :, 128 * n + 128:640])
                wsc[n, :, 128 * n + 128:640] = w
                for i in range(n + 1, 4):
                    other = asc[n, :, 128 * i:128 * i + 128].T
                    asc[i, :, 128 * i:640] = asc[i, :, 128 * i:640] - mm(other, w[:, 128 * (i - n - 1):])
        return carry

    lax.fori_loop(0, 4, eliminate, 0)
    for k in reversed(range(4)):
        y = wsc[k, :, 512:640]
        if k < 3:
            y = y - mm(wsc[k, :, 128 * k + 128:512], xcol[128 * k + 128:512, :])
        xcol[128 * k:128 * k + 128, :] = y


def kernel(
    x_hbm, cc_hbm, dif, vel, cells_hbm, count, value_hbm, scale_hbm, pred_hbm, mean_hbm, obs_hbm, mix_hbm,
    x_ref, cc_ref, cells, value_ref, scale_ref, pred, mean_out, obs_out, mix_out, s_in, s_out,
    turn, a_buf, b_buf, coef, perm, pbf, clsf, cce, hsend, hrecv, wv, wrecv, sbuf, samples,
    fpart, rcore, rplane, zsend, zrecv, fin, ff, asc, wsc, inv, xcol, rows, fields, owned, opart, line,
    s_halo, r_halo, s_cls, r_cls, s_w, r_w, s_s, r_s, s_c, r_c, s_p, r_p, s_z, r_z, s_g, r_g, s_a, r_a, s_b, r_b,
    s_f, r_f, s_o, r_o, s_l, r_l, s_q, r_q, relay,
):
    g, m = place()
    z, xl = g % 16, g // 16
    core = m % 2
    p = plane_of(g, m)
    other = m + 1 - 2 * core
    sender = g // 2 == m
    crossing = jnp.logical_or(g == 15, g == 16)
    barrier = pltpu.get_barrier_semaphore()

    def z_peer(d):
        return xl * 16 + (z + d) % 16, m

    arrays = ((x_hbm, x_ref), (cc_hbm, cc_ref), (cells_hbm, cells), (value_hbm, value_ref), (scale_hbm, scale_ref))
    loads = [pltpu.make_async_copy(a, b, s_in.at[i]) for i, (a, b) in enumerate(arrays)]
    for load in loads:
        load.start()
    arrays = ((pred, pred_hbm), (mean_out, mean_hbm), (obs_out, obs_hbm), (mix_out, mix_hbm))
    stores = [pltpu.make_async_copy(a, b, s_out.at[i]) for i, (a, b) in enumerate(arrays)]

    signal(barrier, z_peer(1))
    signal(barrier, z_peer(15))

    @pl.when(crossing)
    def _():
        signal(barrier, (31 - g, m))

    def greet(d, carry):
        signal(barrier, (g, (m + d) % 16))
        signal(barrier, plane_peer((p + d) % 16, g, m))
        return carry

    lax.fori_loop(1, 16, greet, 0)

    at_row = lax.broadcasted_iota(jnp.int32, (NC, 128), 0)
    at_col = lax.broadcasted_iota(jnp.int32, (NC, 128), 1)
    for t in range(8):
        perm[:, t * 128:(t + 1) * 128] = (at_row == at_col * 8 + t).astype(F32).astype(BF16)
    loads[0].wait()
    loads[1].wait()
    both = jnp.concatenate([x_ref[...].reshape(512, NC), cc_ref[...].astype(F32).astype(BF16)], axis=0)
    for t in range(8):
        moved = jnp.dot(both, perm[:, t * 128:(t + 1) * 128], preferred_element_type=F32)
        turn[t] = moved[0:512]
        clsf[:, t * 128:(t + 1) * 128] = moved[512:528]

    def shuffle(r, carry):
        for q in range(4):
            for t in range(8):
                a_buf[q, r + HALO, :, t * 128:(t + 1) * 128] = turn[t, pl.ds(q * 128 + r, 8, stride=16), :]
        return carry

    lax.fori_loop(0, 16, shuffle, 0)
    for side in range(2):
        def pack(r, carry, side=side):
            for h in range(2):
                pair = [a_buf[2 * h + i, r + HALO + side * 10] for i in range(2)]
                hsend[side, h, r] = jnp.concatenate(pair, axis=0).astype(BF16)
            return carry

        lax.fori_loop(0, HALO, pack, 0)

    pl.semaphore_wait(barrier, 32 + crossing.astype(jnp.int32))

    def up(h):
        return remote(hsend.at[0, h], hrecv.at[1, h], s_halo.at[0, h], r_halo.at[1, h], (g - 1, m))

    def down(h):
        return remote(hsend.at[1, h], hrecv.at[0, h], s_halo.at[1, h], r_halo.at[0, h], (g + 1, m))

    cup = remote(clsf.at[pl.ds(0, 8)], cce.at[pl.ds(24, 8)], s_cls.at[0], r_cls.at[1], (g - 1, m))
    cdown = remote(clsf.at[pl.ds(8, 8)], cce.at[pl.ds(0, 8)], s_cls.at[1], r_cls.at[0], (g + 1, m))

    @pl.when(g > 0)
    def _():
        cup.start()
        up(0).start()

    @pl.when(g < 31)
    def _():
        cdown.start()
        down(0).start()

    def tell(k):
        signal(relay.at[k], z_peer(2**k))
        signal(relay.at[k], z_peer(16 - 2**k))

    tell(0)
    cce[pl.ds(8, 16), :] = clsf[...]
    fill_coefs((1, 2), g, cce, dif, vel, coef)

    @pl.when(g == 0)
    def _():
        hrecv[0] = jnp.zeros((2, HALO, 16, NC), BF16)
        cce[pl.ds(0, 8), :] = jnp.zeros((8, NC), F32)

    @pl.when(g == 31)
    def _():
        hrecv[1] = jnp.zeros((2, HALO, 16, NC), BF16)
        cce[pl.ds(24, 8), :] = jnp.zeros((8, NC), F32)

    bufs = (a_buf, b_buf)

    def edge(src, q, r):
        return pltpu.roll(src[q, r, :, 7 * 128:], 1, 1), pltpu.roll(src[q, r, :, :128], 127, 1)

    def advance(k, r, members):
        src, dst = bufs[k % 2], bufs[(k + 1) % 2]
        done = []
        for q in members:
            mid = [src[q, r, :, t * 128:(t + 1) * 128] for t in range(8)]
            first, last = edge(src, q, r)
            tiles = []
            for t in range(8):
                lanes = slice(t * 128, (t + 1) * 128)
                c = [jnp.broadcast_to(coef[t, r + 2, i:i + 1, :], (8, 128)) for i in range(5)]
                left = mid[t - 1] if t else first
                right = mid[t + 1] if t < 7 else last
                out = c[0] * mid[t]
                out = out + c[1] * src[q, r - 1, :, lanes] + c[2] * src[q, r + 1, :, lanes]
                out = out + c[3] * left + c[4] * right
                if k < STEPS - 1:
                    dst[q, r, :, lanes] = out
                tiles.append(out)
            done.append(jnp.concatenate(tiles, axis=1))
        if k == STEPS - 1:
            for h in range(len(members) // 2):
                pair = jnp.concatenate(done[2 * h:2 * h + 2], axis=0).astype(BF16)
                pbf[members[2 * h] // 2, r - HALO] = pair

    pl.semaphore_wait(relay.at[0], 2)
    tell(1)

    for k in range(STEPS):
        def inner(r, carry, k=k):
            advance(k, r, (0, 1, 2, 3))
            return carry

        lax.fori_loop(HALO + 1 + k, EXT - HALO - 1 - k, inner, 0, unroll=2)
        if k == 1:
            pl.semaphore_wait(relay.at[1], 2)
            tell(2)

            @pl.when(g > 0)
            def _():
                up(1).start()

            @pl.when(g < 31)
            def _():
                down(1).start()

    pl.semaphore_wait(relay.at[2], 2)
    signal(relay.at[3], (g + 16 - 32 * xl, m))

    for load in loads[2:]:
        load.wait()
    slot = lax.broadcasted_iota(jnp.int32, (1, 128), 1)
    for s in range(32):
        valid = (slot < count[0, s]).astype(F32)
        wv[s] = jnp.concatenate([scale_ref[0, s:s + 1, :] * valid, value_ref[0, s:s + 1, :]], axis=1)

    def give_weights():
        @pl.when(sender)
        def _():
            def give(d, carry):
                s = (g + d) % 32
                remote(wv.at[s], wrecv.at[g % 2], s_w.at[d], r_w.at[g % 2], (s, m)).start()
                return carry

            lax.fori_loop(1, 32, give, 0)
            wrecv[g % 2] = wv[g]

    pl.semaphore_wait(relay.at[3], 1)
    give_weights()

    @pl.when(g > 0)
    def _():
        cup.wait_send()
        cdown.wait_recv()

    @pl.when(g < 31)
    def _():
        cdown.wait_send()
        cup.wait_recv()

    fill_coefs((0, 3), g, cce, dif, vel, coef)

    at_place = lax.broadcasted_iota(jnp.int32, (256, 256), 0)

    def sample(chunk):
        cell = jnp.concatenate([cells[0, pl.ds(2 * chunk + i, 1), :] for i in range(2)], axis=1)
        spot = across(cell % NC)
        key = (cell // NC) * 4 + spot // 256
        onehot = (at_place == spot % 256).astype(F32).astype(BF16)
        state = pbf[...].reshape(512, NC)
        tall = jnp.concatenate([state[:, 256 * b:256 * b + 256] for b in range(4)], axis=0)
        wide = jnp.dot(tall, onehot, preferred_element_type=F32)
        total = [jnp.zeros((16, 256), F32), jnp.zeros((16, 256), F32)]
        for r in range(16):
            for b in range(4):
                hit = key == r * 4 + b
                for h in range(2):
                    at = b * 512 + h * 256 + r * 16
                    total[h] = total[h] + jnp.where(hit, wide[at:at + 16], 0.0)
        sbuf[chunk] = jnp.concatenate(total, axis=0).astype(BF16)

    for h in range(2):
        @pl.when(g > 0)
        def _(h=h):
            up(h).wait_send()
            down(h).wait_recv()

        @pl.when(g < 31)
        def _(h=h):
            down(h).wait_send()
            up(h).wait_recv()

        for side in range(2):
            def widen(r, carry, side=side, h=h):
                rows = hrecv[side, h, r].astype(F32)
                a_buf[2 * h, r + side * 22] = rows[0:8]
                a_buf[2 * h + 1, r + side * 22] = rows[8:16]
                return carry

            lax.fori_loop(0, HALO, widen, 0)
        for k in range(STEPS):
            def outer_rows(i, carry, k=k, h=h):
                advance(k, k + 1 + i, (2 * h, 2 * h + 1))
                advance(k, EXT - 2 - k - i, (2 * h, 2 * h + 1))
                return carry

            lax.fori_loop(0, HALO, outer_rows, 0, unroll=2)

    def scatter(e, carry):
        k = (e // 2) % 4
        step = jnp.where(k < 2, 2 + k, 3 - k)
        peer = ((m // 8 + 1 - e // 8) % 2) * 8 + ((m // 2 + step) % 4) * 2 + (m + 1 + e) % 2
        sample(peer)
        remote(sbuf.at[peer], samples.at[m], s_s.at[peer], r_s.at[m], (g, peer)).start()
        return carry

    lax.fori_loop(0, 15, scatter, 0)
    sample(m)
    samples[m] = sbuf[m]

    def scattered(d, carry):
        peer = (m + d) % 16
        c = remote(sbuf.at[peer], samples.at[peer], s_s.at[peer], r_s.at[peer], (g, peer))
        c.wait_send()
        c.wait_recv()
        return carry

    lax.fori_loop(1, 16, scattered, 0)

    @pl.when(sender)
    def _():
        def given(d, carry):
            remote(wv.at[g], wrecv.at[g % 2], s_w.at[d], r_w.at[g % 2], (g, m)).wait_send()
            return carry

        lax.fori_loop(1, 32, given, 0)

    for o in range(2):
        @pl.when(2 * m + o != g)
        def _(o=o):
            remote(wv.at[g], wrecv.at[o], s_w.at[0], r_w.at[o], (g, m)).wait_recv()

    sampled = samples[...].reshape(MEMBERS, 256).astype(F32)
    mean = jnp.sum(sampled, axis=0, keepdims=True) / MEMBERS
    weight = jnp.concatenate([wrecv[0, :, 0:128], wrecv[1, :, 0:128]], axis=1)
    value = jnp.concatenate([wrecv[0, :, 128:256], wrecv[1, :, 128:256]], axis=1)
    panel = ((sampled - mean) * weight).astype(BF16)
    parts = split3((value - mean) * weight)
    line_at = lax.broadcasted_iota(jnp.int32, (128, 256), 0)
    dep_one = jnp.zeros((128, 256), F32)
    dep_two = jnp.zeros((128, 256), F32)
    for i in range(3):
        dep_one = jnp.where(line_at == i, parts[i].astype(F32), dep_one)
        dep_two = jnp.where(line_at == 64 + i, parts[i].astype(F32), dep_two)
    dep_one = dep_one.astype(BF16)
    dep_two = dep_two.astype(BF16)
    blk = [panel[i * 128:(i + 1) * 128] for i in range(4)]

    def outer(a, b):
        return lax.dot_general(a, b, (((1,), (1,)), ((), ())), preferred_element_type=F32)

    pairs = (
        ((0, 0), (0, 1), (0, 2), (0, 3), (3, 3)),
        ((1, 1), (1, 2), (1, 3), (2, 2), (2, 3)),
    )
    for h in range(2):
        for t in range(5):
            i, j = pairs[h][t]
            fpart[h, :, t] = outer(blk[i], blk[j]).reshape(16, 8, 128)
        fpart[h, :, 5] = (outer(blk[h], dep_one) + outer(blk[3 - h], dep_two)).reshape(16, 8, 128)

    swap = remote(fpart.at[1 - core], rcore, s_c.at[0], r_c.at[0], (g, other))
    swap.start()
    swap.wait()

    def pair_sum(i, carry):
        rcore[i] = rcore[i] + fpart[core, i]
        return carry

    lax.fori_loop(0, 16, pair_sum, 0)

    def plane_give(d, carry):
        q = (p + d) % 16
        remote(rcore.at[q], rplane.at[p], s_p.at[d], r_p.at[p], plane_peer(q, g, m)).start()
        return carry

    lax.fori_loop(1, 16, plane_give, 0)

    flat = pbf[...].reshape(512, NC)
    for t in range(8):
        back = lax.dot_general(
            flat, perm[t * 128:(t + 1) * 128, :], (((1,), (1,)), ((), ())), preferred_element_type=F32
        )
        rows[:, :, :, t * 128:(t + 1) * 128] = back.astype(BF16).reshape(2, 16, 16, 128)
        for h in range(2):
            for r in range(16):
                for q in range(2):
                    at = h * 256 + r * 16 + q * 8
                    turn[t, pl.ds((2 * h + q) * 128 + r, 8, stride=16), :] = back[at:at + 8]

    def finish(i, carry):
        for t in range(8):
            pred[i, :, t * 128:(t + 1) * 128] = turn[t, pl.ds(i * 16, 16), :].astype(BF16)
        return carry

    lax.fori_loop(0, 32, finish, 0)
    stores[0].start()

    def plane_take(d, total):
        q = (p + d) % 16
        remote(rcore.at[q], rplane.at[q], s_p.at[d], r_p.at[q], plane_peer(q, g, m)).wait_recv()
        return total + rplane[q]

    zsend[...] = lax.fori_loop(1, 16, plane_take, rcore[p])

    def field_give(d, carry):
        q = (m + d) % 16
        remote(rows.at[:, q], fields.at[m], s_f.at[d], r_f.at[m], (g, q)).start()
        return carry

    lax.fori_loop(1, 16, field_give, 0)
    fields[m] = rows[:, m]
    for j in range(6):
        @pl.when(z != z_reducer(j))
        def _(j=j):
            remote(zsend.at[j], zrecv.at[z], s_z.at[j], r_z.at[z], (xl * 16 + z_reducer(j), m)).start()

    for j in range(6):
        @pl.when(z == z_reducer(j))
        def _(j=j):
            def z_take(d, total):
                q = (z + d) % 16
                remote(zsend.at[j], zrecv.at[q], s_z.at[j], r_z.at[q], (xl * 16 + q, m)).wait_recv()
                return total + zrecv[q]

            fin[p, j] = lax.fori_loop(1, 16, z_take, zsend[j])

            def z_give(d, carry):
                q = (z + d) % 16
                remote(fin.at[p, j], fin.at[p, j], s_g.at[d], r_g.at[j], (xl * 16 + q, m)).start()
                return carry

            lax.fori_loop(1, 16, z_give, 0)

    for j in range(6):
        @pl.when(z != z_reducer(j))
        def _(j=j):
            remote(fin.at[p, j], fin.at[p, j], s_g.at[0], r_g.at[j], (xl * 16 + z_reducer(j), m)).wait_recv()

    def plane_send(d, carry):
        q = (p + d) % 16
        remote(fin.at[p], fin.at[p], s_a.at[d], r_a.at[p], plane_peer(q, g, m)).start()
        return carry

    lax.fori_loop(1, 16, plane_send, 0)

    def own_give(d, carry):
        o = (g + d) % 32
        lanes = pl.ds(pl.multiple_of((o % 2) * 128, 128), 128)
        remote(sbuf.at[o // 2, :, lanes], owned.at[g], s_o.at[d], r_o.at[g], (o, m)).start()
        return carry

    lax.fori_loop(1, 32, own_give, 0)
    owned[g] = sbuf[g // 2, :, pl.ds(pl.multiple_of((g % 2) * 128, 128), 128)]

    def home(q):
        return remote(fin.at[q], ff.at[core, q], s_b.at[q], r_b.at[q], (g, other))

    home(p).start()
    ff[core, p] = fin[p]

    def plane_got(d, carry):
        q = (p + d) % 16
        remote(fin.at[q], fin.at[q], s_a.at[d], r_a.at[q], plane_peer(q, g, m)).wait_recv()
        home(q).start()
        ff[core, q] = fin[q]
        return carry

    lax.fori_loop(1, 16, plane_got, 0)

    def homed(q, carry):
        home(q).wait_send()
        remote(fin.at[q], ff.at[1 - core, q], s_b.at[q], r_b.at[q], (g, other)).wait_recv()
        return carry

    lax.fori_loop(0, 16, homed, 0)

    solve(ff, asc, wsc, inv, xcol)

    x = xcol[...]
    shift = 1.0 / MEMBERS - jnp.sum(x[:, 0:1], axis=0, keepdims=True) / MEMBERS
    coefs = []
    for k in range(4):
        piece = x[k * 128:(k + 1) * 128].T[0:8, :]
        mix_out[:, k * 128:(k + 1) * 128] = piece[0:1]
        coefs.append(piece + shift)
    pieces = split3(jnp.concatenate(coefs, axis=1))

    def weigh(array):
        total = jnp.zeros((8, array.shape[1]), F32)
        for piece in pieces:
            total = total + jnp.dot(piece, array, preferred_element_type=F32)
        return total[0:1]

    mine = xcol[pl.ds(pl.multiple_of(m * 32, 32), 32), :] + shift

    def own_take(d, carry):
        o = (g + d) % 32
        lanes = pl.ds(pl.multiple_of((o % 2) * 128, 128), 128)
        c = remote(sbuf.at[o // 2, :, lanes], owned.at[o], s_o.at[d], r_o.at[o], (o, m))
        c.wait_send()
        c.wait_recv()
        return carry

    lax.fori_loop(1, 32, own_take, 0)
    sums = [jnp.sum(mine * owned[s].astype(F32), axis=0, keepdims=True) for s in range(32)]
    opart[m] = jnp.concatenate(sums, axis=0)

    def part_give(d, carry):
        q = (m + d) % 16
        remote(opart.at[m], opart.at[m], s_q.at[d], r_q.at[m], (g, q)).start()
        return carry

    lax.fori_loop(1, 16, part_give, 0)

    def field_take(d, carry):
        q = (m + d) % 16
        c = remote(rows.at[:, q], fields.at[q], s_f.at[d], r_f.at[q], (g, q))
        c.wait_send()
        c.wait_recv()
        return carry

    lax.fori_loop(1, 16, field_take, 0)
    line[m] = weigh(fields[...].reshape(MEMBERS, NC))

    def line_give(d, carry):
        q = (m + d) % 16
        remote(line.at[m], line.at[m], s_l.at[d], r_l.at[m], (g, q)).start()
        return carry

    lax.fori_loop(1, 16, line_give, 0)

    def drain(d, carry):
        q = (p + d) % 16
        remote(rcore.at[q], rplane.at[q], s_p.at[d], r_p.at[q], plane_peer(q, g, m)).wait_send()
        remote(fin.at[p], fin.at[p], s_a.at[d], r_a.at[p], plane_peer(q, g, m)).wait_send()
        return carry

    lax.fori_loop(1, 16, drain, 0)
    for j in range(6):
        @pl.when(z != z_reducer(j))
        def _(j=j):
            remote(zsend.at[j], zrecv.at[z], s_z.at[j], r_z.at[z], (xl * 16 + z_reducer(j), m)).wait_send()

        @pl.when(z == z_reducer(j))
        def _(j=j):
            def z_given(d, carry):
                q = (z + d) % 16
                remote(fin.at[p, j], fin.at[p, j], s_g.at[d], r_g.at[j], (xl * 16 + q, m)).wait_send()
                return carry

            lax.fori_loop(1, 16, z_given, 0)

    def line_take(d, carry):
        q = (m + d) % 16
        c = remote(line.at[m], line.at[q], s_l.at[d], r_l.at[q], (g, q))
        c.wait_send()
        c.wait_recv()
        return carry

    lax.fori_loop(1, 16, line_take, 0)

    mean_out[...] = jnp.concatenate([line[r] for r in range(16)], axis=0)

    def part_take(d, carry):
        q = (m + d) % 16
        c = remote(opart.at[m], opart.at[q], s_q.at[d], r_q.at[q], (g, q))
        c.wait_send()
        c.wait_recv()
        return carry

    lax.fori_loop(1, 16, part_take, 0)
    total = opart[0]
    for q in range(1, 16):
        total = total + opart[q]
    obs_out[...] = total
    for store in stores[1:]:
        store.start()

    for store in stores:
        store.wait()


def local(
    prior_sample_matrix, cell_class, diffusion_table, velocity_table, obs_cells, obs_count, obs_value, obs_scale
):
    hbm = pl.BlockSpec(memory_space=pl.ANY)
    smem = pl.BlockSpec(memory_space=pltpu.SMEM)
    dma = pltpu.SemaphoreType.DMA
    pred, mean, obs, mix = pl.pallas_call(
        kernel,
        out_shape=(
            jax.ShapeDtypeStruct((32, 16, NC), BF16),
            jax.ShapeDtypeStruct((16, NC), F32),
            jax.ShapeDtypeStruct((32, 128), F32),
            jax.ShapeDtypeStruct((1, MEMBERS), F32),
        ),
        in_specs=[hbm, hbm, smem, smem, hbm, smem, hbm, hbm],
        out_specs=(hbm, hbm, hbm, hbm),
        scratch_shapes=[
            pltpu.VMEM((32, 16, NC), BF16),
            pltpu.VMEM((16, NC), jnp.int32),
            pltpu.VMEM((1, 32, 128), jnp.int32),
            pltpu.VMEM((1, 32, 128), F32),
            pltpu.VMEM((1, 32, 128), F32),
            pltpu.VMEM((32, 16, NC), BF16),
            pltpu.VMEM((16, NC), F32),
            pltpu.VMEM((32, 128), F32),
            pltpu.VMEM((1, MEMBERS), F32),
            dma((5,)),
            dma((4,)),
            pltpu.VMEM((8, 512, 128), F32),
            pltpu.VMEM((4, EXT, 8, NC), F32),
            pltpu.VMEM((4, EXT, 8, NC), F32),
            pltpu.VMEM((8, 32, 8, 128), F32),
            pltpu.VMEM((NC, NC), BF16),
            pltpu.VMEM((2, 16, 16, NC), BF16),
            pltpu.VMEM((16, NC), F32),
            pltpu.VMEM((32, NC), F32),
            pltpu.VMEM((2, 2, HALO, 16, NC), BF16),
            pltpu.VMEM((2, 2, HALO, 16, NC), BF16),
            pltpu.VMEM((32, 1, 256), F32),
            pltpu.VMEM((2, 1, 256), F32),
            pltpu.VMEM((16, 32, 256), BF16),
            pltpu.VMEM((16, 32, 256), BF16),
            pltpu.VMEM((2, 16, 6, 8, 128), F32),
            pltpu.VMEM((16, 6, 8, 128), F32),
            pltpu.VMEM((16, 6, 8, 128), F32),
            pltpu.VMEM((6, 8, 128), F32),
            pltpu.VMEM((16, 8, 128), F32),
            pltpu.VMEM((16, 6, 8, 128), F32),
            pltpu.VMEM((2, 16, 6, 8, 128), F32),
            pltpu.VMEM((4, 128, 640), F32),
            pltpu.VMEM((4, 128, 640), F32),
            pltpu.VMEM((128, 128), F32),
            pltpu.VMEM((MEMBERS, 128), F32),
            pltpu.VMEM((2, 16, 16, NC), BF16),
            pltpu.VMEM((16, 2, 16, NC), BF16),
            pltpu.VMEM((32, 32, 128), BF16),
            pltpu.VMEM((16, 32, 128), F32),
            pltpu.VMEM((16, 1, NC), F32),
            dma((2, 2)), dma((2, 2)), dma((2,)), dma((2,)), dma((32,)), dma((2,)), dma((16,)), dma((16,)),
            dma((1,)), dma((1,)), dma((16,)), dma((16,)), dma((6,)), dma((16,)), dma((16,)), dma((6,)),
            dma((16,)), dma((16,)), dma((16,)), dma((16,)),
            dma((16,)), dma((16,)), dma((32,)), dma((32,)), dma((16,)), dma((16,)),
            dma((16,)), dma((16,)),
            pltpu.SemaphoreType.REGULAR((4,)),
        ],
        compiler_params=pltpu.CompilerParams(
            collective_id=0, has_side_effects=True, vmem_limit_bytes=VMEM_LIMIT
        ),
    )(prior_sample_matrix, cell_class, diffusion_table, velocity_table, obs_cells, obs_count, obs_value, obs_scale)
    return pred, mean, obs.reshape(1, 32, 128), mix.reshape(MEMBERS)


def solution(mesh):
    in_specs = (
        P("member", "grid", None),
        P("grid", None),
        P(),
        P(),
        P("grid", None, None),
        P("grid", None),
        P("grid", None, None),
        P("grid", None, None),
    )
    out_specs = (P("member", "grid", None), P("grid", None), P("grid", None, None), P())
    return jax.shard_map(local, mesh=mesh, in_specs=in_specs, out_specs=out_specs, check_vma=False)
```
